32 devices in a mesh: groups: 2 (over y), gx: 4 (over x, core), gy: 4 (over z).
Axes of the slice: x: 2, y: 2, z: 4, core: 2. Of those that a mesh axis runs over, the one named last changes fastest.
Arguments:
- hidden_states: bfloat16 [512, 16384], P(('groups', 'gx'), 'gy'), parts along dimension 0, may hold values from -36 to 36
- norm_gain: bfloat16 [16384], P('gy'), may hold values from 0.5 to 1.5
- projection_weight: bfloat16 [16384, 18432], P('gy', 'gx'), may hold values from -0.046875 to 0.046875
- key_cache: bfloat16 [512, 128, 1024], P(('groups', 'gx', 'gy')), parts along dimension 0, may hold values from -250 to 250
- value_cache: bfloat16 [512, 128, 1024], P(('groups', 'gx', 'gy')), parts along dimension 0, may hold values from -4 to 4
- lengths: int32 [512], P(('groups', 'gx', 'gy')), parts along dimension 0, may hold values from 1 to 128, as said below
Outputs:
- attended: bfloat16 [512, 16384], P(('groups', 'gx', 'gy')), parts along dimension 0
- new_cache_rows: bfloat16 [512, 2048], P(('groups', 'gx', 'gy')), parts along dimension 0
The draws below stay inside these ranges and needn't reach their ends.
There are 2 independent parts, one for each index of `groups`. The reference program is written for one: setup_inputs(seed, part) draws one part's arguments, and reference() takes and returns one part's arrays. A program takes and returns all parts, laid end to end along the dimension named above; an argument that names none is the same for every part. Nothing has to cross between parts.
Inputs may be any that keep to these rules, and one draw needn't show every extreme that they name: Row r holds cached keys and values at positions 0 to lengths[r] - 1, and its new token stands at position lengths[r]; the first of every 128 rows has length 128.
All inputs are finite; a program needn't handle non-finite values.
Results may differ from the reference program's by a relative error of at most 0.012.
Values may be sent and summed in bfloat16 or wider, within the bound.
No kernel may reach another device: no remote copies, remote signals or barrier semaphores. Data moves between devices by JAX's collectives and lax.ppermute only.
A program may use at most 128 MiB of HBM per device.

```python
import math
import jax
import jax.numpy as jnp
from jax import lax

D = 16384
HEADS = 128
KV_HEADS = 8
HEAD_DIM = 128
ROWS_DEV = 16
CACHE = 128
ROWS = 256


def log_spread(key, shape, low, high):
    return jnp.exp(jax.random.uniform(key, shape, jnp.float32, math.log(low), math.log(high)))


def draw_hidden_states(key, part):
    key = jax.random.fold_in(key, 1)
    base_key, row_key, column_key = jax.random.split(key, 3)
    base = jnp.clip(jax.random.normal(base_key, (ROWS, D), jnp.float32), -4.0, 4.0)
    row_scale = log_spread(row_key, (ROWS, 1), 0.3, 3.0)
    column_scale = log_spread(column_key, (1, D), 0.3, 3.0)
    return (base * row_scale * column_scale).astype(jnp.bfloat16)


def draw_key_cache(key, part):
    key = jax.random.fold_in(key, 2)
    width = KV_HEADS * HEAD_DIM
    base = jnp.clip(jax.random.normal(key, (ROWS, CACHE, width), jnp.float32), -4.0, 4.0)
    return base.astype(jnp.bfloat16)


def draw_lengths(key, part):
    key = jax.random.fold_in(key, 3)
    front_key, second_key = jax.random.split(key)
    front = jax.random.randint(front_key, (ROWS,), 0, CACHE)
    second = jax.random.randint(second_key, (ROWS,), 0, CACHE)
    drawn = 1 + front * second // CACHE
    places = jnp.arange(ROWS, dtype=jnp.int32)
    return jnp.where(places % (8 * ROWS_DEV) == 0, CACHE, drawn).astype(jnp.int32)


def shard_levels(rng, dims, pieces, least, high):
    gain = 1.0
    for dim, shards_of in pieces:
        steps = jax.random.uniform(jax.random.fold_in(jax.random.fold_in(rng, 6), dim), (shards_of,), jnp.float32, least / len(pieces), high / len(pieces))
        gain = gain * jnp.repeat(jnp.exp(steps), dims[dim] // shards_of).reshape((-1,) + (1,) * (len(dims) - 1 - dim))
    return gain


def noise(rng, shape, deviation, most, cuts=(), held_as=jnp.bfloat16):
    array = deviation * jax.random.normal(rng, shape, jnp.float32)
    if cuts:
        array = array * shard_levels(rng, shape, cuts, -0.22, 0.18)
    return jnp.clip(array, -most, most).astype(held_as)


def setup_inputs(seed: int = 0, part: int = 0) -> dict:
    splits = jax.random.split(jax.random.key(seed), 7)
    part_splits = jax.random.split(jax.random.fold_in(splits[6], part), 7)
    hidden_states = draw_hidden_states(jax.random.fold_in(jax.random.fold_in(splits[6], part), 71), part)
    norm_gain = jnp.clip(1.0 + 0.1 * jax.random.normal(splits[1], (D,), jnp.float32), 0.5, 1.5).astype(jnp.bfloat16)
    projection_weight = noise(splits[2], (D, (HEADS + 2 * KV_HEADS) * HEAD_DIM), D ** -0.5, 0.046875, ((0, 4), (1, 4)))
    key_cache = draw_key_cache(jax.random.fold_in(jax.random.fold_in(splits[6], part), 71), part)
    value_cache = noise(part_splits[4], (ROWS, CACHE, KV_HEADS * HEAD_DIM), 1.0, 4.0, ((0, 16),))
    lengths = draw_lengths(jax.random.fold_in(jax.random.fold_in(splits[6], part), 71), part)
    return dict(hidden_states=hidden_states, norm_gain=norm_gain, projection_weight=projection_weight, key_cache=key_cache, value_cache=value_cache, lengths=lengths)


norm_eps = 1e-05
rope_base = 500000.0

def rotate_heads(heads, position):
    half_dim = heads.shape[-1] // 2
    freq_steps = jnp.arange(half_dim, dtype=jnp.float32)
    inverse = jnp.exp(freq_steps * (-2.0 * math.log(rope_base) / heads.shape[-1]))
    angles = position[:, None, None] * inverse[None, None, :]
    cosine = jnp.cos(angles)
    sine = jnp.sin(angles)
    front = heads[..., :half_dim]
    second = heads[..., half_dim:]
    return jnp.concatenate([front * cosine - second * sine, second * cosine + front * sine], axis=-1)

def finish_rows(projected, key_cache, value_cache, lengths):
    row_count = projected.shape[0]
    cache_span = key_cache.shape[1]
    group_size = HEADS // KV_HEADS
    query_width = HEADS * HEAD_DIM
    key_width = KV_HEADS * HEAD_DIM
    position = lengths.astype(jnp.float32)
    query_heads = projected[:, :query_width].astype(jnp.float32).reshape(row_count, HEADS, HEAD_DIM)
    key_heads = projected[:, query_width:query_width + key_width].astype(jnp.float32).reshape(row_count, KV_HEADS, HEAD_DIM)
    value_heads = projected[:, query_width + key_width:]
    queries = rotate_heads(query_heads, position).astype(jnp.bfloat16)
    new_key = rotate_heads(key_heads, position).astype(jnp.bfloat16)
    new_cache_rows = jnp.concatenate([new_key.reshape(row_count, key_width), value_heads], axis=1)
    grouped = queries.reshape(row_count, KV_HEADS, group_size, HEAD_DIM).astype(jnp.float32)
    shaped_keys = key_cache.reshape(row_count, cache_span, KV_HEADS, HEAD_DIM).astype(jnp.float32)
    shaped_values = value_cache.reshape(row_count, cache_span, KV_HEADS, HEAD_DIM).astype(jnp.float32)
    scale = HEAD_DIM ** (-0.5)
    scores = jnp.einsum('rkgd,rlkd->rkgl', grouped, shaped_keys) * scale
    own_score = jnp.einsum('rkgd,rkd->rkg', grouped, new_key.astype(jnp.float32)) * scale
    usable = jnp.arange(cache_span, dtype=jnp.int32)[None, :] < lengths[:, None]
    masked = jnp.where(usable[:, None, None, :], scores, -jnp.inf)
    top_score = jnp.maximum(lax.optimization_barrier(jnp.max(masked, axis=3)), own_score)
    raised = jnp.exp(masked - top_score[..., None])
    raised_own = jnp.exp(own_score - top_score)
    totals = lax.optimization_barrier(jnp.sum(raised, axis=3)) + raised_own
    weights = (raised / totals[..., None]).astype(jnp.bfloat16)
    own_weight = (raised_own / totals).astype(jnp.bfloat16)
    mixed = jnp.einsum('rkgl,rlkd->rkgd', weights.astype(jnp.float32), shaped_values)
    own_values = value_heads.astype(jnp.float32).reshape(row_count, KV_HEADS, HEAD_DIM)
    mixed = mixed + own_weight.astype(jnp.float32)[..., None] * own_values[:, :, None, :]
    attended = mixed.reshape(row_count, HEADS * HEAD_DIM).astype(jnp.bfloat16)
    return (attended, new_cache_rows)

def reference(hidden_states, norm_gain, projection_weight, key_cache, value_cache, lengths):
    values_in = hidden_states.astype(jnp.float32)
    square = lax.optimization_barrier(jnp.sum(values_in * values_in, axis=1))
    normed = (values_in * norm_gain.astype(jnp.float32)[None, :]).astype(jnp.bfloat16)
    summed = jnp.dot(normed, projection_weight, preferred_element_type=jnp.float32)
    projected = (summed * lax.rsqrt(square / D + norm_eps)[:, None]).astype(jnp.bfloat16)
    group_count = ROWS // ROWS_DEV

    def one_group(items):
        return finish_rows(items[0], items[1], items[2], items[3])
    attended, new_cache_rows = lax.map(one_group, (projected.reshape(group_count, ROWS_DEV, projected.shape[1]), key_cache.reshape(group_count, ROWS_DEV, CACHE, KV_HEADS * HEAD_DIM), value_cache.reshape(group_count, ROWS_DEV, CACHE, KV_HEADS * HEAD_DIM), lengths.reshape(group_count, ROWS_DEV)))
    return (attended.reshape(ROWS, HEADS * HEAD_DIM), new_cache_rows.reshape(ROWS, 2 * KV_HEADS * HEAD_DIM))
```

```python
import functools
import math

import jax
import jax.numpy as jnp
from jax import lax
from jax.experimental import pallas as pl
from jax.experimental.pallas import tpu as pltpu
from jax.sharding import PartitionSpec as P

D = 16384
HEADS = 128
KV_HEADS = 8
HEAD_DIM = 128
GROUP = HEADS // KV_HEADS
CORES = 2

norm_eps = 1e-05
rope_base = 500000.0
f32 = jnp.float32
bf16 = jnp.bfloat16


def prep_kernel(order, rows, z_ref, hidden_ref, gain_ref, normed_ref):
    gain = gain_ref[...].astype(f32)
    for place, m in enumerate(order):
        start = pl.multiple_of(jnp.bitwise_xor(z_ref[0], m) * rows, rows)
        block = hidden_ref[pl.ds(start, rows), :].astype(f32)
        normed_ref[pl.ds(place * rows, rows), :] = (block * gain).astype(bf16)


def prepare(hidden, gain, z, order, rows):
    return pl.pallas_call(
        functools.partial(prep_kernel, order, rows),
        out_shape=jax.ShapeDtypeStruct(hidden.shape, bf16),
        in_specs=[
            pl.BlockSpec(memory_space=pltpu.SMEM),
            pl.BlockSpec(memory_space=pltpu.VMEM),
            pl.BlockSpec(memory_space=pltpu.VMEM),
        ],
        out_specs=pl.BlockSpec(memory_space=pltpu.VMEM),
        name="prepare",
    )(z, hidden, gain.reshape(1, -1))


def project_kernel(half, a0_ref, a1_ref, w_ref, keep_ref, send_ref):
    rows = jnp.concatenate([a0_ref[...], a1_ref[...]], axis=0)
    total = jnp.dot(rows, w_ref[...], preferred_element_type=f32)
    for j in range(CORES):
        keep_ref[pl.ds(j * half, half), :] = total[2 * j * half : (2 * j + 1) * half]
        send_ref[pl.ds(j * half, half), :] = total[(2 * j + 1) * half : (2 * j + 2) * half].astype(bf16)


def project(a0, a1, weight, first, width):
    rows, depth = a0.shape
    tile = next(t for t in (256, 384, 128) if width % t == 0 and first % t == 0)
    begin = first // tile
    return pl.pallas_call(
        functools.partial(project_kernel, rows // 2),
        grid=(width // tile,),
        out_shape=(
            jax.ShapeDtypeStruct((rows, width), f32),
            jax.ShapeDtypeStruct((rows, width), bf16),
        ),
        in_specs=[
            pl.BlockSpec((rows, depth), lambda i: (0, 0)),
            pl.BlockSpec((rows, depth), lambda i: (0, 0)),
            pl.BlockSpec((depth, tile), lambda i: (0, begin + i)),
        ],
        out_specs=(
            pl.BlockSpec((rows, tile), lambda i: (0, i)),
            pl.BlockSpec((rows, tile), lambda i: (0, i)),
        ),
        compiler_params=pltpu.CompilerParams(vmem_limit_bytes=32 * 2**20),
        name="project",
    )(a0, a1, weight)


def attend_kernel(plan, rows, per_source, *refs):
    count = sum(len(parts) for _, _, _, parts in plan)
    places_ref, lengths_ref, square_ref, cosine_ref, sine_ref = refs[:5]
    pieces = refs[5 : 5 + count]
    keys_hbm, values_hbm, attended_ref, cache_rows_ref = refs[5 + count : 9 + count]
    keys, values, table, heads, mixed, sems = refs[9 + count :]
    copies = []
    for r in range(rows):
        pair = (
            pltpu.make_async_copy(keys_hbm.at[r], keys.at[r], sems.at[0, r]),
            pltpu.make_async_copy(values_hbm.at[r], values.at[r], sems.at[1, r]),
        )
        for copy in pair:
            copy.start()
        copies.append(pair)
    at = 0
    for source, first, width, parts in plan:
        total = pieces[at][...].astype(f32)
        for other in range(1, len(parts)):
            total = total + pieces[at + other][...].astype(f32)
        at += len(parts)
        table[places_ref[source], :, pl.ds(first, width)] = total
    scale_rows = lax.rsqrt(square_ref[...] * (1.0 / D) + norm_eps)
    cosine = cosine_ref[...]
    sine = sine_ref[...]
    for h in range(HEADS + 2 * KV_HEADS):
        column = (h % per_source) * HEAD_DIM
        head = table[h // per_source, :, pl.ds(column, HEAD_DIM)] * scale_rows
        head = head.astype(bf16)
        if h < HEADS + KV_HEADS:
            head = head.astype(f32)
            head = (head * cosine + pltpu.roll(head, HEAD_DIM // 2, 1) * sine).astype(bf16)
        if h >= HEADS:
            cache_rows_ref[:, pl.ds((h - HEADS) * HEAD_DIM, HEAD_DIM)] = head
        heads[pl.ds(h * rows, rows), :] = head.astype(f32)
    span = keys.shape[1]
    position = lax.broadcasted_iota(jnp.int32, (HEADS, span), 1)
    for r in range(rows):
        for copy in copies[r]:
            copy.wait()
        query = heads[pl.ds(r, HEADS, stride=rows), :]
        own_key = heads[pl.ds(HEADS * rows + r, KV_HEADS, stride=rows), :]
        own_value = heads[pl.ds((HEADS + KV_HEADS) * rows + r, KV_HEADS, stride=rows), :]
        spread = jnp.concatenate(
            [jnp.broadcast_to(own_key[k : k + 1], (GROUP, HEAD_DIM)) for k in range(KV_HEADS)], axis=0
        )
        own_score = jnp.sum(query * spread, axis=1, keepdims=True) * HEAD_DIM ** (-0.5)
        query = query.astype(bf16)
        scores = jnp.concatenate(
            [
                lax.dot_general(
                    query[k * GROUP : (k + 1) * GROUP],
                    keys[r, :, pl.ds(k * HEAD_DIM, HEAD_DIM)],
                    (((1,), (1,)), ((), ())),
                    preferred_element_type=f32,
                )
                for k in range(KV_HEADS)
            ],
            axis=0,
        ) * HEAD_DIM ** (-0.5)
        masked = jnp.where(position < lengths_ref[r], scores, -jnp.inf)
        top = jnp.maximum(jnp.max(masked, axis=1, keepdims=True), own_score)
        raised = jnp.exp(masked - top)
        raised_own = jnp.exp(own_score - top)
        inverse = 1.0 / (jnp.sum(raised, axis=1, keepdims=True) + raised_own)
        weights = (raised * inverse).astype(bf16)
        own_weight = (raised_own * inverse).astype(bf16).astype(f32)
        result = jnp.concatenate(
            [
                jnp.dot(
                    weights[k * GROUP : (k + 1) * GROUP],
                    values[r, :, pl.ds(k * HEAD_DIM, HEAD_DIM)],
                    preferred_element_type=f32,
                )
                + own_weight[k * GROUP : (k + 1) * GROUP] * own_value[k : k + 1]
                for k in range(KV_HEADS)
            ],
            axis=0,
        )
        mixed[pl.ds(r, HEADS, stride=rows), :] = result
    for h in range(HEADS):
        attended_ref[:, pl.ds(h * HEAD_DIM, HEAD_DIM)] = mixed[pl.ds(h * rows, rows), :].astype(bf16)


def attend(plan, pieces, places, lengths, square, cosine, sine, key_cache, value_cache, sources, width):
    rows, span, kv_width = key_cache.shape
    smem = pl.BlockSpec(memory_space=pltpu.SMEM)
    vmem = pl.BlockSpec(memory_space=pltpu.VMEM)
    hbm = pl.BlockSpec(memory_space=pl.ANY)
    return pl.pallas_call(
        functools.partial(attend_kernel, plan, rows, width // HEAD_DIM),
        out_shape=(
            jax.ShapeDtypeStruct((rows, HEADS * HEAD_DIM), bf16),
            jax.ShapeDtypeStruct((rows, 2 * KV_HEADS * HEAD_DIM), bf16),
        ),
        in_specs=[smem, smem, vmem, vmem, vmem] + [vmem] * len(pieces) + [hbm, hbm],
        out_specs=(vmem, vmem),
        scratch_shapes=[
            pltpu.VMEM((rows, span, kv_width), bf16),
            pltpu.VMEM((rows, span, kv_width), bf16),
            pltpu.VMEM((sources, rows, width), f32),
            pltpu.VMEM(((HEADS + 2 * KV_HEADS) * rows, HEAD_DIM), f32),
            pltpu.VMEM((HEADS * rows, HEAD_DIM), f32),
            pltpu.SemaphoreType.DMA((2, rows)),
        ],
        compiler_params=pltpu.CompilerParams(vmem_limit_bytes=40 * 2**20),
        name="attend",
    )(places, lengths, square, cosine, sine, *pieces, key_cache, value_cache)


def rotation(lengths):
    half = HEAD_DIM // 2
    steps = jnp.arange(half, dtype=f32)
    inverse = jnp.exp(steps * (-2.0 * math.log(rope_base) / HEAD_DIM))
    angles = lengths.astype(f32)[:, None] * inverse[None, :]
    cosine = jnp.cos(angles)
    sine = jnp.sin(angles)
    return jnp.concatenate([cosine, cosine], axis=1), jnp.concatenate([-sine, sine], axis=1)


def body(hidden_states, norm_gain, projection_weight, key_cache, value_cache, lengths):
    along_x = lax.axis_size("gx")
    along_z = lax.axis_size("gy")
    chips = along_x // CORES
    rows = key_cache.shape[0]
    width = projection_weight.shape[1]
    z = lax.axis_index("gy")
    gx = lax.axis_index("gx")
    order = list(range(0, along_z, 2)) + list(range(1, along_z, 2))
    kept = along_z // 2

    def on_gx(array, shift, flip):
        pairs = [
            ((x + shift) % chips * CORES + (c ^ flip), x * CORES + c)
            for x in range(chips)
            for c in range(CORES)
        ]
        return lax.ppermute(array, "gx", pairs)

    def on_z(array, flip):
        return lax.ppermute(array, "gy", [(s, s ^ flip) for s in range(along_z)])

    def deliver(array, shift, flip, m):
        pairs = [
            (
                (x * CORES + c) * along_z + s,
                ((x + shift) % chips * CORES + (c ^ flip)) * along_z + (s ^ m),
            )
            for x in range(chips)
            for c in range(CORES)
            for s in range(along_z)
        ]
        return lax.ppermute(array, ("gx", "gy"), pairs)

    normed = prepare(hidden_states, norm_gain, z.reshape(1).astype(jnp.int32), order, rows)
    here = [(normed, on_gx(normed, 0, 1))]
    for k in range(1, chips):
        there = on_gx(normed, k, 0)
        here.append((there, on_gx(there, 0, 1)))

    local = hidden_states.astype(f32)
    square = jnp.sum(local * local, axis=1).reshape(along_z, rows)
    square = jnp.concatenate(
        [lax.dynamic_slice_in_dim(square, jnp.bitwise_xor(z, m), 1, axis=0) for m in order], axis=0
    )
    square = square[:kept] + on_z(square[kept:], 1)
    square = sum(
        [on_z(square[i : i + 1], 2 * i) for i in range(1, kept)], square[:1]
    ).reshape(rows, 1)
    cosine, sine = rotation(lengths)

    cut = 2 if width % (2 * HEAD_DIM) == 0 else 1
    chunk = width // cut
    plan = []
    pieces = []
    for k in range(chips):
        for c in range(cut):
            keep, send = project(*here[k], projection_weight, c * chunk, chunk)
            both = (keep + on_z(send, 1).astype(f32)).astype(bf16).reshape(CORES, kept, rows, chunk)
            for j in range(CORES):
                parts = []
                for i in range(kept):
                    part = both[j, i]
                    if k or j or i:
                        part = deliver(part, k, j, 2 * i)
                    parts.append(part)
                plan.append((k * CORES + j, c * chunk, chunk, tuple(range(len(parts)))))
                pieces.extend(parts)
    x, core = gx // CORES, gx % CORES
    places = jnp.stack(
        [
            (x + chips - k) % chips * CORES + jnp.bitwise_xor(core, j)
            for k in range(chips)
            for j in range(CORES)
        ]
    ).astype(jnp.int32)
    return attend(
        plan, pieces, places, lengths, square, cosine, sine, key_cache, value_cache, along_x, width
    )


def solution(mesh):
    in_specs = (
        P(("groups", "gx"), "gy"),
        P("gy"),
        P("gy", "gx"),
        P(("groups", "gx", "gy"), None, None),
        P(("groups", "gx", "gy"), None, None),
        P(("groups", "gx", "gy")),
    )
    out_specs = (P(("groups", "gx", "gy"), None), P(("groups", "gx", "gy"), None))
    return jax.shard_map(body, mesh=mesh, in_specs=in_specs, out_specs=out_specs, check_vma=False)
```

```python
import functools
import math

import jax
import jax.numpy as jnp
from jax import lax
from jax.experimental import pallas as pl
from jax.experimental.pallas import tpu as pltpu
from jax.sharding import PartitionSpec as P

D = 16384
HEADS = 128
KV_HEADS = 8
HEAD_DIM = 128
GROUP = HEADS // KV_HEADS
CORES = 2

norm_eps = 1e-05
rope_base = 500000.0
f32 = jnp.float32
bf16 = jnp.bfloat16


def project_kernel(rows, kept, first, tiles, squared, z_ref, a0_ref, a1_ref, gain_ref, w_hbm, keep_ref, send_ref, raw, acts, w, row_sems, w_sems):
    copies = []
    for at, (begin, width) in enumerate(tiles):
        copies.append(
            pltpu.make_async_copy(
                w_hbm.at[:, pl.ds(first + begin, width)], w.at[:, pl.ds(begin, width)], w_sems.at[at]
            )
        )
    half = kept * CORES * rows
    loads = []
    for m in range(2 * kept):
        source = pl.multiple_of(jnp.bitwise_xor(z_ref[0], m) * rows, rows)
        for j, ref in enumerate((a0_ref, a1_ref)):
            place = (m % 2) * half + ((m // 2) * CORES + j) * rows
            load = pltpu.make_async_copy(
                ref.at[pl.ds(source, rows), :], raw.at[pl.ds(place, rows), :], row_sems.at[m * CORES + j]
            )
            load.start()
            loads.append((place, load))
    for copy in copies:
        copy.start()
    gain = gain_ref[...].astype(f32)
    side = lax.broadcasted_iota(jnp.int32, (rows, HEAD_DIM), 1) < HEAD_DIM // 2
    offset = HEAD_DIM if squared else 0
    for place, load in loads:
        load.wait()
        block = raw[pl.ds(place, rows), :].astype(f32)
        acts[pl.ds(place, rows), :] = (block * gain).astype(bf16)
        if squared:
            square = jnp.broadcast_to(jnp.sum(block * block, axis=1, keepdims=True), (rows, HEAD_DIM))
            square = split(square, side)
            if place < half:
                keep_ref[pl.ds(place, rows), pl.ds(0, HEAD_DIM)] = square
            else:
                send_ref[pl.ds(place - half, rows), pl.ds(0, HEAD_DIM)] = square.astype(bf16)
    for copy, (begin, width) in zip(copies, tiles):
        copy.wait()
        total = jnp.dot(acts[...], w[:, pl.ds(begin, width)], preferred_element_type=f32)
        keep_ref[:, pl.ds(offset + begin, width)] = total[:half]
        send_ref[:, pl.ds(offset + begin, width)] = total[half:].astype(bf16)


def split(square, side):
    upper = square.astype(bf16).astype(f32)
    return jnp.where(side, upper, square - upper)


def joined(parts):
    return parts + pltpu.roll(parts, HEAD_DIM // 2, 1)


def project(z, a0, a1, gain, weight, rows, first, width, squared):
    depth = a0.shape[1]
    kept = a0.shape[0] // rows // 2
    half = kept * CORES * rows
    size = 512
    tiles = tuple((b, min(size, width - b)) for b in range(0, width, size))
    full = width + (HEAD_DIM if squared else 0)
    vmem = pl.BlockSpec(memory_space=pltpu.VMEM)
    hbm = pl.BlockSpec(memory_space=pl.ANY)
    return pl.pallas_call(
        functools.partial(project_kernel, rows, kept, first, tiles, squared),
        out_shape=(
            jax.ShapeDtypeStruct((half, full), f32),
            jax.ShapeDtypeStruct((half, full), bf16),
        ),
        in_specs=[pl.BlockSpec(memory_space=pltpu.SMEM), hbm, hbm, vmem, pl.BlockSpec(memory_space=pltpu.HBM)],
        out_specs=(vmem, vmem),
        scratch_shapes=[
            pltpu.VMEM((2 * half, depth), bf16),
            pltpu.VMEM((2 * half, depth), bf16),
            pltpu.VMEM((depth, width), bf16),
            pltpu.SemaphoreType.DMA((2 * kept * CORES,)),
            pltpu.SemaphoreType.DMA((len(tiles),)),
        ],
        compiler_params=pltpu.CompilerParams(vmem_limit_bytes=36 * 2**20),
        name="project",
    )(z, a0, a1, gain, weight)


def pair_kernel(widths, squared, first_rows, *refs):
    count = len(widths)
    keeps, receiveds = refs[:count], refs[count : 2 * count]
    own_ref, away_ref = refs[2 * count :]
    begin = 0
    for at, (keep, received, width) in enumerate(zip(keeps, receiveds, widths)):
        source = 0
        if squared and at == 0:
            side = lax.broadcasted_iota(jnp.int32, (keep.shape[0], HEAD_DIM), 1) < HEAD_DIM // 2
            columns = pl.ds(0, HEAD_DIM)
            total = split(joined(keep[:, columns] + received[:, columns].astype(f32)), side)
            own_ref[:, columns] = total[:first_rows]
            away_ref[:, columns] = total[first_rows:].astype(bf16)
            source = HEAD_DIM
            begin = HEAD_DIM
        columns = pl.ds(source, width)
        total = keep[:, columns] + received[:, columns].astype(f32)
        own_ref[:, pl.ds(begin, width)] = total[:first_rows]
        away_ref[:, pl.ds(begin, width)] = total[first_rows:].astype(bf16)
        begin += width


def pair_sums(keeps, receiveds, widths, squared, first_rows):
    full = sum(widths) + (HEAD_DIM if squared else 0)
    vmem = pl.BlockSpec(memory_space=pltpu.VMEM)
    return pl.pallas_call(
        functools.partial(pair_kernel, tuple(widths), squared, first_rows),
        out_shape=(
            jax.ShapeDtypeStruct((first_rows, full), f32),
            jax.ShapeDtypeStruct((keeps[0].shape[0] - first_rows, full), bf16),
        ),
        in_specs=[vmem] * (2 * len(widths)),
        out_specs=(vmem, vmem),
        name="pair_sums",
    )(*keeps, *receiveds)


def finish_kernel(squared, *refs):
    if squared:
        own, *others, projected_ref, scale_ref = refs
        columns = pl.ds(0, HEAD_DIM)
        square = joined(own[:, columns])
        for other in others:
            square = square + joined(other[:, columns].astype(f32))
        scale = lax.rsqrt(square * (1.0 / D) + norm_eps)
        scale_ref[...] = scale
        start = HEAD_DIM
    else:
        own, *others, scale_in, projected_ref = refs
        scale = scale_in[...]
        start = 0
    for begin in range(0, projected_ref.shape[1], HEAD_DIM):
        columns = pl.ds(start + begin, HEAD_DIM)
        total = own[:, columns]
        for other in others:
            total = total + other[:, columns].astype(f32)
        projected_ref[:, pl.ds(begin, HEAD_DIM)] = (total * scale).astype(bf16)


def finish(own, others, scale):
    squared = scale is None
    rows, full = own.shape
    width = full - (HEAD_DIM if squared else 0)
    vmem = pl.BlockSpec(memory_space=pltpu.VMEM)
    shapes = [jax.ShapeDtypeStruct((rows, width), bf16)]
    if squared:
        shapes.append(jax.ShapeDtypeStruct((rows, HEAD_DIM), f32))
    inputs = [own, *others] + ([] if squared else [scale])
    results = pl.pallas_call(
        functools.partial(finish_kernel, squared),
        out_shape=tuple(shapes),
        in_specs=[vmem] * len(inputs),
        out_specs=(vmem,) * len(shapes),
        name="finish",
    )(*inputs)
    return (results[0], results[1] if squared else scale)


def attend_kernel(plan, rows, per_source, *refs):
    count = len(plan)
    places_ref, lengths_ref, cosine_ref, sine_ref = refs[:4]
    pieces = refs[4 : 4 + count]
    keys_hbm, values_hbm, attended_ref, cache_rows_ref = refs[4 + count : 8 + count]
    keys, values, table, heads, mixed, sems = refs[8 + count :]
    copies = []
    for r in range(rows):
        pair = (
            pltpu.make_async_copy(keys_hbm.at[r], keys.at[r], sems.at[0, r]),
            pltpu.make_async_copy(values_hbm.at[r], values.at[r], sems.at[1, r]),
        )
        for copy in pair:
            copy.start()
        copies.append(pair)
    for (source, first, width, start), piece in zip(plan, pieces):
        table[places_ref[source], :, pl.ds(first, width)] = piece[pl.ds(start, rows), :].astype(f32)
    cosine = cosine_ref[...]
    sine = sine_ref[...]
    for h in range(HEADS + 2 * KV_HEADS):
        column = (h % per_source) * HEAD_DIM
        head = table[h // per_source, :, pl.ds(column, HEAD_DIM)]
        if h < HEADS + KV_HEADS:
            head = head * cosine + pltpu.roll(head, HEAD_DIM // 2, 1) * sine
        head = head.astype(bf16)
        if h >= HEADS:
            cache_rows_ref[:, pl.ds((h - HEADS) * HEAD_DIM, HEAD_DIM)] = head
        heads[pl.ds(h * rows, rows), :] = head.astype(f32)
    span = keys.shape[1]
    position = lax.broadcasted_iota(jnp.int32, (HEADS, span), 1)
    for r in range(rows):
        for copy in copies[r]:
            copy.wait()
        query = heads[pl.ds(r, HEADS, stride=rows), :]
        own_key = heads[pl.ds(HEADS * rows + r, KV_HEADS, stride=rows), :]
        own_value = heads[pl.ds((HEADS + KV_HEADS) * rows + r, KV_HEADS, stride=rows), :]
        spread = jnp.concatenate(
            [jnp.broadcast_to(own_key[k : k + 1], (GROUP, HEAD_DIM)) for k in range(KV_HEADS)], axis=0
        )
        own_score = jnp.sum(query * spread, axis=1, keepdims=True) * HEAD_DIM ** (-0.5)
        query = query.astype(bf16)
        scores = jnp.concatenate(
            [
                lax.dot_general(
                    query[k * GROUP : (k + 1) * GROUP],
                    keys[r, :, pl.ds(k * HEAD_DIM, HEAD_DIM)],
                    (((1,), (1,)), ((), ())),
                    preferred_element_type=f32,
                )
                for k in range(KV_HEADS)
            ],
            axis=0,
        ) * HEAD_DIM ** (-0.5)
        masked = jnp.where(position < lengths_ref[r], scores, -jnp.inf)
        top = jnp.maximum(jnp.max(masked, axis=1, keepdims=True), own_score)
        raised = jnp.exp(masked - top)
        raised_own = jnp.exp(own_score - top)
        inverse = 1.0 / (jnp.sum(raised, axis=1, keepdims=True) + raised_own)
        weights = (raised * inverse).astype(bf16)
        own_weight = (raised_own * inverse).astype(bf16).astype(f32)
        result = jnp.concatenate(
            [
                jnp.dot(
                    weights[k * GROUP : (k + 1) * GROUP],
                    values[r, :, pl.ds(k * HEAD_DIM, HEAD_DIM)],
                    preferred_element_type=f32,
                )
                + own_weight[k * GROUP : (k + 1) * GROUP] * own_value[k : k + 1]
                for k in range(KV_HEADS)
            ],
            axis=0,
        )
        mixed[pl.ds(r, HEADS, stride=rows), :] = result
    for h in range(HEADS):
        attended_ref[:, pl.ds(h * HEAD_DIM, HEAD_DIM)] = mixed[pl.ds(h * rows, rows), :].astype(bf16)


def attend(plan, pieces, places, lengths, cosine, sine, key_cache, value_cache, sources, width):
    rows, span, kv_width = key_cache.shape
    smem = pl.BlockSpec(memory_space=pltpu.SMEM)
    vmem = pl.BlockSpec(memory_space=pltpu.VMEM)
    hbm = pl.BlockSpec(memory_space=pltpu.HBM)
    return pl.pallas_call(
        functools.partial(attend_kernel, plan, rows, width // HEAD_DIM),
        out_shape=(
            jax.ShapeDtypeStruct((rows, HEADS * HEAD_DIM), bf16),
            jax.ShapeDtypeStruct((rows, 2 * KV_HEADS * HEAD_DIM), bf16),
        ),
        in_specs=[smem, smem, vmem, vmem] + [vmem] * len(pieces) + [hbm, hbm],
        out_specs=(vmem, vmem),
        scratch_shapes=[
            pltpu.VMEM((rows, span, kv_width), bf16),
            pltpu.VMEM((rows, span, kv_width), bf16),
            pltpu.VMEM((sources, rows, width), f32),
            pltpu.VMEM(((HEADS + 2 * KV_HEADS) * rows, HEAD_DIM), f32),
            pltpu.VMEM((HEADS * rows, HEAD_DIM), f32),
            pltpu.SemaphoreType.DMA((2, rows)),
        ],
        compiler_params=pltpu.CompilerParams(vmem_limit_bytes=40 * 2**20),
        name="attend",
    )(places, lengths, cosine, sine, *pieces, key_cache, value_cache)


def rotation(lengths):
    half = HEAD_DIM // 2
    steps = jnp.arange(half, dtype=f32)
    inverse = jnp.exp(steps * (-2.0 * math.log(rope_base) / HEAD_DIM))
    angles = lengths.astype(f32)[:, None] * inverse[None, :]
    cosine = jnp.cos(angles)
    sine = jnp.sin(angles)
    return jnp.concatenate([cosine, cosine], axis=1), jnp.concatenate([-sine, sine], axis=1)


def body(hidden_states, norm_gain, projection_weight, key_cache, value_cache, lengths):
    along_x = lax.axis_size("gx")
    along_z = lax.axis_size("gy")
    chips = along_x // CORES
    rows = key_cache.shape[0]
    width = projection_weight.shape[1]
    z = lax.axis_index("gy").reshape(1).astype(jnp.int32)
    gx = lax.axis_index("gx")
    kept = along_z // 2
    first_rows = CORES * rows

    def on_gx(array, shift, flip):
        pairs = [
            ((x + shift) % chips * CORES + (c ^ flip), x * CORES + c)
            for x in range(chips)
            for c in range(CORES)
        ]
        return lax.ppermute(array, "gx", pairs)

    def on_z(array, flip):
        return lax.ppermute(array, "gy", [(s, s ^ flip) for s in range(along_z)])

    gain = norm_gain.reshape(1, -1)
    there = [on_gx(hidden_states, k, 0) for k in range(1, chips)]
    here = [(hidden_states, on_gx(hidden_states, 0, 1))]
    for array in there:
        here.append((array, on_gx(array, 0, 1)))
    cosine, sine = rotation(lengths)

    unit = HEAD_DIM * 2
    if width % unit == 0 and width >= 4 * unit:
        cuts = {0: split_at(width, unit, 0.5), 1: split_at(width, unit, 0.6)}
    else:
        cuts = {0: (width,), 1: (width,)}
    plan = []
    pieces = []
    before = None
    for k in range(chips):
        chunks = cuts[min(k, 1)]
        a0, a1 = here[k]
        keeps = []
        receiveds = []
        first = 0
        groups = []
        for c, chunk in enumerate(chunks):
            if before is not None and c == 1:
                a0, before = lax.optimization_barrier((a0, before))
            keep, send = project(z, a0, a1, gain, projection_weight, rows, first, chunk, c == 0)
            first += chunk
            keeps.append(keep)
            receiveds.append(on_z(send, 1))
        if k == 0:
            groups = [list(range(len(chunks)))]
        else:
            groups = [[c] for c in range(len(chunks))]
        scale = None
        first = 0
        for group in groups:
            own, away = pair_sums(
                [keeps[c] for c in group],
                [receiveds[c] for c in group],
                [chunks[c] for c in group],
                scale is None,
                first_rows,
            )
            if k == 0:
                before = away
            others = [
                on_z(away if kept == 2 else away[(i - 1) * first_rows : i * first_rows], 2 * i)
                for i in range(1, kept)
            ]
            projected, scale = finish(own, others, scale)
            if k:
                projected = on_gx(projected, chips - k, 0)
            size = projected.shape[1]
            plan.append((k * CORES, first, size, 0))
            pieces.append(projected)
            plan.append((k * CORES + 1, first, size, rows))
            pieces.append(on_gx(projected, 0, 1))
            first += size
    x, core = gx // CORES, gx % CORES
    places = jnp.stack(
        [
            (x + chips - k) % chips * CORES + jnp.bitwise_xor(core, j)
            for k in range(chips)
            for j in range(CORES)
        ]
    ).astype(jnp.int32)
    return attend(plan, pieces, places, lengths, cosine, sine, key_cache, value_cache, along_x, width)


def split_at(width, unit, share):
    first = round(width * share / unit) * unit
    return (first, width - first)


def solution(mesh):
    in_specs = (
        P(("groups", "gx"), "gy"),
        P("gy"),
        P("gy", "gx"),
        P(("groups", "gx", "gy"), None, None),
        P(("groups", "gx", "gy"), None, None),
        P(("groups", "gx", "gy")),
    )
    out_specs = (P(("groups", "gx", "gy"), None), P(("groups", "gx", "gy"), None))
    return jax.shard_map(body, mesh=mesh, in_specs=in_specs, out_specs=out_specs, check_vma=False)
```

```python
import functools
import math

import jax
import jax.numpy as jnp
from jax import lax
from jax.experimental import pallas as pl
from jax.experimental.pallas import tpu as pltpu
from jax.sharding import PartitionSpec as P

D = 16384
HEADS = 128
KV_HEADS = 8
HEAD_DIM = 128
GROUP = HEADS // KV_HEADS
CORES = 2
IN_FLIGHT = 2

norm_eps = 1e-05
rope_base = 500000.0
f32 = jnp.float32
bf16 = jnp.bfloat16


def project_kernel(rows, kept, first, tiles, squared, z_ref, a0_ref, a1_ref, gain_ref, w_hbm, keep_hbm, send_ref, raw, acts, w, keep, row_sems, w_sems, keep_sems):
    half = kept * CORES * rows
    loads = []
    for m in range(2 * kept):
        source = pl.multiple_of(jnp.bitwise_xor(z_ref[0], m) * rows, rows)
        for j, ref in enumerate((a0_ref, a1_ref)):
            place = (m % 2) * half + ((m // 2) * CORES + j) * rows
            load = pltpu.make_async_copy(
                ref.at[pl.ds(source, rows), :], raw.at[pl.ds(place, rows), :], row_sems.at[m * CORES + j]
            )
            load.start()
            loads.append((place, load))
    copies = [
        pltpu.make_async_copy(
            w_hbm.at[:, pl.ds(first + begin, width)], w.at[:, pl.ds(begin, width)], w_sems.at[at]
        )
        for at, (begin, width) in enumerate(tiles)
    ]
    for copy in copies[:IN_FLIGHT]:
        copy.start()
    gain = gain_ref[...].astype(f32)
    offset = HEAD_DIM if squared else 0
    for place, load in loads:
        load.wait()
        block = raw[pl.ds(place, rows), :].astype(f32)
        acts[pl.ds(place, rows), :] = (block * gain).astype(bf16)
        if squared:
            square = jnp.broadcast_to(jnp.sum(block * block, axis=1, keepdims=True), (rows, HEAD_DIM))
            if place < half:
                keep[pl.ds(place, rows), pl.ds(0, HEAD_DIM)] = square
            else:
                upper = square.astype(bf16)
                send_ref[pl.ds(place - half, rows), pl.ds(0, HEAD_DIM)] = upper
                lower = (square - upper.astype(f32)).astype(bf16)
                send_ref[pl.ds(place - half, rows), pl.ds(HEAD_DIM, HEAD_DIM)] = lower
    stores = []
    for at, (copy, (begin, width)) in enumerate(zip(copies, tiles)):
        copy.wait()
        if at + IN_FLIGHT < len(copies):
            copies[at + IN_FLIGHT].start()
        total = jnp.dot(acts[...], w[:, pl.ds(begin, width)], preferred_element_type=f32)
        keep[:, pl.ds(offset + begin, width)] = total[:half]
        send_ref[:, pl.ds(2 * offset + begin, width)] = total[half:].astype(bf16)
        left = 0 if at == 0 else offset + begin
        columns = pl.ds(left, offset + begin + width - left)
        store = pltpu.make_async_copy(keep.at[:, columns], keep_hbm.at[:, columns], keep_sems.at[at])
        store.start()
        stores.append(store)
    for store in stores:
        store.wait()


def tiles_of(width):
    sizes = []
    while width:
        size = min(512, width) if width >= 1024 or width % 256 else 256
        sizes.append(size)
        width -= size
    return tuple((sum(sizes[:i]), size) for i, size in enumerate(sizes))


def project(z, a0, a1, gain, weight, rows, first, width, squared):
    depth = a0.shape[1]
    kept = a0.shape[0] // rows // 2
    half = kept * CORES * rows
    tiles = tiles_of(width)
    full = width + (HEAD_DIM if squared else 0)
    vmem = pl.BlockSpec(memory_space=pltpu.VMEM)
    hbm = pl.BlockSpec(memory_space=pltpu.HBM)
    return pl.pallas_call(
        functools.partial(project_kernel, rows, kept, first, tiles, squared),
        out_shape=(
            jax.ShapeDtypeStruct((half, full), f32),
            jax.ShapeDtypeStruct((half, 2 * full - width), bf16),
        ),
        in_specs=[pl.BlockSpec(memory_space=pltpu.SMEM), hbm, hbm, vmem, hbm],
        out_specs=(hbm, vmem),
        scratch_shapes=[
            pltpu.VMEM((2 * half, depth), bf16),
            pltpu.VMEM((2 * half, depth), bf16),
            pltpu.VMEM((depth, width), bf16),
            pltpu.VMEM((half, full), f32),
            pltpu.SemaphoreType.DMA((2 * kept * CORES,)),
            pltpu.SemaphoreType.DMA((len(tiles),)),
            pltpu.SemaphoreType.DMA((len(tiles),)),
        ],
        compiler_params=pltpu.CompilerParams(vmem_limit_bytes=32 * 2**20),
        name="project",
    )(z, a0, a1, gain, weight)


def attend_kernel(plan, rows, per_source, *refs):
    count = len(plan)
    places_ref, lengths_ref, cosine_ref, sine_ref = refs[:4]
    pieces = refs[4 : 4 + count]
    keys_hbm, values_hbm, attended_ref, cache_rows_ref = refs[4 + count : 8 + count]
    keys, values, table, heads, mixed, piece_sems, sems = refs[8 + count :]
    fills = []
    for at, ((source, first, width, start), piece) in enumerate(zip(plan, pieces)):
        fill = pltpu.make_async_copy(
            piece.at[pl.ds(start, rows), :], table.at[places_ref[source], :, pl.ds(first, width)], piece_sems.at[at]
        )
        fill.start()
        fills.append(fill)
    batch = 4
    copies = []
    for at in range(0, rows, batch):
        span = pl.ds(at, batch)
        copies.append(pltpu.make_async_copy(keys_hbm.at[span], keys.at[span], sems.at[0, at // batch]))
        copies.append(pltpu.make_async_copy(values_hbm.at[span], values.at[span], sems.at[1, at // batch]))
    for copy in copies:
        copy.start()
    for fill in fills:
        fill.wait()
    cosine = cosine_ref[...]
    sine = sine_ref[...]
    for h in range(HEADS + 2 * KV_HEADS):
        column = (h % per_source) * HEAD_DIM
        head = table[h // per_source, :, pl.ds(column, HEAD_DIM)].astype(f32)
        if h < HEADS + KV_HEADS:
            head = head * cosine + pltpu.roll(head, HEAD_DIM // 2, 1) * sine
        head = head.astype(bf16)
        if h >= HEADS:
            cache_rows_ref[:, pl.ds((h - HEADS) * HEAD_DIM, HEAD_DIM)] = head
        heads[pl.ds(h * rows, rows), :] = head.astype(f32)
    span = keys.shape[1]
    position = lax.broadcasted_iota(jnp.int32, (HEADS, span), 1)
    for r in range(rows):
        if r % batch == 0:
            copies[r // batch * 2].wait()
            copies[r // batch * 2 + 1].wait()
        query = heads[pl.ds(r, HEADS, stride=rows), :]
        own_key = heads[pl.ds(HEADS * rows + r, KV_HEADS, stride=rows), :]
        own_value = heads[pl.ds((HEADS + KV_HEADS) * rows + r, KV_HEADS, stride=rows), :]
        spread = jnp.concatenate(
            [jnp.broadcast_to(own_key[k : k + 1], (GROUP, HEAD_DIM)) for k in range(KV_HEADS)], axis=0
        )
        own_score = jnp.sum(query * spread, axis=1, keepdims=True) * HEAD_DIM ** (-0.5)
        query = query.astype(bf16)
        scores = jnp.concatenate(
            [
                lax.dot_general(
                    query[k * GROUP : (k + 1) * GROUP],
                    keys[r, :, pl.ds(k * HEAD_DIM, HEAD_DIM)],
                    (((1,), (1,)), ((), ())),
                    preferred_element_type=f32,
                )
                for k in range(KV_HEADS)
            ],
            axis=0,
        ) * HEAD_DIM ** (-0.5)
        masked = jnp.where(position < lengths_ref[r], scores, -jnp.inf)
        top = jnp.maximum(jnp.max(masked, axis=1, keepdims=True), own_score)
        raised = jnp.exp(masked - top)
        raised_own = jnp.exp(own_score - top)
        inverse = 1.0 / (jnp.sum(raised, axis=1, keepdims=True) + raised_own)
        weights = (raised * inverse).astype(bf16)
        own_weight = (raised_own * inverse).astype(bf16).astype(f32)
        result = jnp.concatenate(
            [
                jnp.dot(
                    weights[k * GROUP : (k + 1) * GROUP],
                    values[r, :, pl.ds(k * HEAD_DIM, HEAD_DIM)],
                    preferred_element_type=f32,
                )
                + own_weight[k * GROUP : (k + 1) * GROUP] * own_value[k : k + 1]
                for k in range(KV_HEADS)
            ],
            axis=0,
        )
        mixed[pl.ds(r, HEADS, stride=rows), :] = result
    for h in range(HEADS):
        attended_ref[:, pl.ds(h * HEAD_DIM, HEAD_DIM)] = mixed[pl.ds(h * rows, rows), :].astype(bf16)


def attend(plan, pieces, places, lengths, cosine, sine, key_cache, value_cache, sources, width):
    rows, span, kv_width = key_cache.shape
    smem = pl.BlockSpec(memory_space=pltpu.SMEM)
    vmem = pl.BlockSpec(memory_space=pltpu.VMEM)
    hbm = pl.BlockSpec(memory_space=pltpu.HBM)
    return pl.pallas_call(
        functools.partial(attend_kernel, plan, rows, width // HEAD_DIM),
        out_shape=(
            jax.ShapeDtypeStruct((rows, HEADS * HEAD_DIM), bf16),
            jax.ShapeDtypeStruct((rows, 2 * KV_HEADS * HEAD_DIM), bf16),
        ),
        in_specs=[smem, smem, vmem, vmem] + [hbm] * len(pieces) + [hbm, hbm],
        out_specs=(vmem, vmem),
        scratch_shapes=[
            pltpu.VMEM((rows, span, kv_width), bf16),
            pltpu.VMEM((rows, span, kv_width), bf16),
            pltpu.VMEM((sources, rows, width), bf16),
            pltpu.VMEM(((HEADS + 2 * KV_HEADS) * rows, HEAD_DIM), f32),
            pltpu.VMEM((HEADS * rows, HEAD_DIM), f32),
            pltpu.SemaphoreType.DMA((len(pieces),)),
            pltpu.SemaphoreType.DMA((2, rows // 4)),
        ],
        compiler_params=pltpu.CompilerParams(vmem_limit_bytes=24 * 2**20),
        name="attend",
    )(places, lengths, cosine, sine, *pieces, key_cache, value_cache)


def rotation(lengths):
    half = HEAD_DIM // 2
    steps = jnp.arange(half, dtype=f32)
    inverse = jnp.exp(steps * (-2.0 * math.log(rope_base) / HEAD_DIM))
    angles = lengths.astype(f32)[:, None] * inverse[None, :]
    cosine = jnp.cos(angles)
    sine = jnp.sin(angles)
    return jnp.concatenate([cosine, cosine], axis=1), jnp.concatenate([-sine, sine], axis=1)


def body(hidden_states, norm_gain, projection_weight, key_cache, value_cache, lengths):
    along_x = lax.axis_size("gx")
    along_z = lax.axis_size("gy")
    chips = along_x // CORES
    rows = key_cache.shape[0]
    width = projection_weight.shape[1]
    z = lax.axis_index("gy").reshape(1).astype(jnp.int32)
    gx = lax.axis_index("gx")
    kept = along_z // 2
    first_rows = CORES * rows

    def on_gx(array, shift, flip):
        pairs = [
            ((x + shift) % chips * CORES + (c ^ flip), x * CORES + c)
            for x in range(chips)
            for c in range(CORES)
        ]
        return lax.ppermute(array, "gx", pairs)

    def on_z(array, flip):
        return lax.ppermute(array, "gy", [(s, s ^ flip) for s in range(along_z)])

    def in_hbm(array):
        return pltpu.with_memory_space_constraint(array, pltpu.HBM)

    gain = norm_gain.reshape(1, -1)
    weight = in_hbm(projection_weight)
    there = [on_gx(hidden_states, k, 0) for k in range(1, chips)]
    here = [(in_hbm(hidden_states), on_gx(hidden_states, 0, 1))]
    cosine, sine = rotation(lengths)

    unit = HEAD_DIM * 2
    if width % unit == 0 and width >= 4 * unit:
        cuts = {0: split_at(width, unit, 0.5), 1: split_at(width, unit, 0.6)}
    else:
        cuts = {0: (width,), 1: (width,)}
    plan = []
    pieces = []

    def after(array, other):
        return lax.optimization_barrier((array, other))[0]

    kinds = range(chips)
    chunks = {k: cuts[min(k, 1)] for k in kinds}
    keeps = {k: [] for k in kinds}
    receiveds = {k: [] for k in kinds}
    aways = {}

    def add_pairs(k):
        owns, away = [], []
        for c, chunk in enumerate(chunks[k]):
            keep, received = keeps[k][c], receiveds[k][c]
            if k and c:
                received = after(received, away[2])
            for part, start in ((owns, 0), (away, first_rows)):
                span = slice(start, start + first_rows) if start == 0 else slice(start, None)
                if c == 0:
                    square = (
                        keep[span, :HEAD_DIM]
                        + received[span, :HEAD_DIM].astype(f32)
                        + received[span, HEAD_DIM : 2 * HEAD_DIM].astype(f32)
                    )
                    if start:
                        upper = lax.reduce_precision(square, 8, 7)
                        part.append(upper.astype(bf16))
                        part.append((square - upper).astype(bf16))
                    else:
                        part.append(square)
                skip = HEAD_DIM if c == 0 else 0
                total = keep[span, skip:] + received[span, 2 * skip :].astype(f32)
                part.append(total.astype(bf16) if start else total)
        if k == 0:
            return owns, [jnp.concatenate(away, axis=1)]
        return owns, [jnp.concatenate(away[:3], axis=1), *away[3:]]

    owns = {}
    for k in kinds:
        if k:
            a0 = after(there[k - 1], keeps[k - 1])
            a1 = on_gx(a0, 0, 1)
        else:
            a0, a1 = here[0]
        first = 0
        for c, chunk in enumerate(chunks[k]):
            if k and c == 1:
                a0 = after(a0, aways[k - 1])
            keep, send = project(z, a0, a1, gain, weight, rows, first, chunk, c == 0)
            first += chunk
            keeps[k].append(keep)
            receiveds[k].append(on_z(send, 1))
        owns[k], aways[k] = add_pairs(k)
    for k in kinds:
        arrived = [
            [on_z(away[(i - 1) * first_rows : i * first_rows], 2 * i) for i in range(1, kept)]
            for away in aways[k]
        ]
        if k + 1 < chips:
            arrived = after(arrived, keeps[k + 1])
        square = owns[k][0]
        for other in arrived[0]:
            square = square + other[:, :HEAD_DIM].astype(f32) + other[:, HEAD_DIM : 2 * HEAD_DIM].astype(f32)
        scale = lax.rsqrt(square[:, :1] * (1.0 / D) + norm_eps)
        done = []
        first = 0
        for c, chunk in enumerate(chunks[k]):
            total = owns[k][c + 1]
            for other in arrived[0] if k == 0 else arrived[c]:
                skip = 2 * HEAD_DIM + first if k == 0 else (2 * HEAD_DIM if c == 0 else 0)
                total = total + other[:, skip : skip + chunk].astype(f32)
            done.append((total * scale).astype(bf16))
            first += chunk
        first = 0
        for projected in [jnp.concatenate(done, axis=1)] if k == 0 else done:
            if k:
                projected = on_gx(projected, chips - k, 0)
            size = projected.shape[1]
            plan.append((k * CORES, first, size, 0))
            pieces.append(projected)
            plan.append((k * CORES + 1, first, size, rows))
            pieces.append(on_gx(projected, 0, 1))
            first += size
    x, core = gx // CORES, gx % CORES
    places = jnp.stack(
        [
            (x + chips - k) % chips * CORES + jnp.bitwise_xor(core, j)
            for k in range(chips)
            for j in range(CORES)
        ]
    ).astype(jnp.int32)
    return attend(
        plan, pieces, places, lengths, cosine, sine, in_hbm(key_cache), in_hbm(value_cache), along_x, width
    )


def split_at(width, unit, share):
    first = round(width * share / unit) * unit
    return (first, width - first)


def solution(mesh):
    in_specs = (
        P(("groups", "gx"), "gy"),
        P("gy"),
        P("gy", "gx"),
        P(("groups", "gx", "gy"), None, None),
        P(("groups", "gx", "gy"), None, None),
        P(("groups", "gx", "gy")),
    )
    out_specs = (P(("groups", "gx", "gy"), None), P(("groups", "gx", "gy"), None))
    return jax.shard_map(body, mesh=mesh, in_specs=in_specs, out_specs=out_specs, check_vma=False)
```

```python
import functools
import math

import jax
import jax.numpy as jnp
from jax import lax
from jax.experimental import pallas as pl
from jax.experimental.pallas import tpu as pltpu
from jax.sharding import PartitionSpec as P

D = 16384
HEADS = 128
KV_HEADS = 8
HEAD_DIM = 128
GROUP = HEADS // KV_HEADS
CORES = 2
IN_FLIGHT = 3

norm_eps = 1e-05
rope_base = 500000.0
f32 = jnp.float32
bf16 = jnp.bfloat16


def project_kernel(rows, kept, first, tiles, squared, z_ref, a0_ref, a1_ref, gain_ref, w_hbm, keep_hbm, send_ref, raw, acts, w, keep, row_sems, w_sems, keep_sems):
    half = kept * CORES * rows
    loads = []
    for m in range(2 * kept):
        source = pl.multiple_of(jnp.bitwise_xor(z_ref[0], m) * rows, rows)
        for j, ref in enumerate((a0_ref, a1_ref)):
            place = (m % 2) * half + ((m // 2) * CORES + j) * rows
            load = pltpu.make_async_copy(
                ref.at[pl.ds(source, rows), :], raw.at[pl.ds(place, rows), :], row_sems.at[m * CORES + j]
            )
            load.start()
            loads.append((place, load))
    copies = [
        pltpu.make_async_copy(
            w_hbm.at[:, pl.ds(first + begin, width)], w.at[:, pl.ds(begin, width)], w_sems.at[at]
        )
        for at, (begin, width) in enumerate(tiles)
    ]
    for copy in copies[:IN_FLIGHT]:
        copy.start()
    gain = gain_ref[...].astype(f32)
    offset = HEAD_DIM if squared else 0
    for place, load in loads:
        load.wait()
        block = raw[pl.ds(place, rows), :].astype(f32)
        acts[pl.ds(place, rows), :] = (block * gain).astype(bf16)
        if squared:
            square = jnp.broadcast_to(jnp.sum(block * block, axis=1, keepdims=True), (rows, HEAD_DIM))
            if place < half:
                keep[pl.ds(place, rows), pl.ds(0, HEAD_DIM)] = square
            else:
                upper = square.astype(bf16)
                send_ref[pl.ds(place - half, rows), pl.ds(0, HEAD_DIM)] = upper
                lower = (square - upper.astype(f32)).astype(bf16)
                send_ref[pl.ds(place - half, rows), pl.ds(HEAD_DIM, HEAD_DIM)] = lower
    stores = []
    for at, (copy, (begin, width)) in enumerate(zip(copies, tiles)):
        copy.wait()
        if at + IN_FLIGHT < len(copies):
            copies[at + IN_FLIGHT].start()
        total = jnp.dot(acts[...], w[:, pl.ds(begin, width)], preferred_element_type=f32)
        keep[:, pl.ds(offset + begin, width)] = total[:half]
        send_ref[:, pl.ds(2 * offset + begin, width)] = total[half:].astype(bf16)
        left = 0 if at == 0 else offset + begin
        columns = pl.ds(left, offset + begin + width - left)
        store = pltpu.make_async_copy(keep.at[:, columns], keep_hbm.at[:, columns], keep_sems.at[at])
        store.start()
        stores.append(store)
    for store in stores:
        store.wait()


def tiles_of(width):
    sizes = [256] if width % 256 == 0 else []
    while width > sum(sizes):
        sizes.append(min(512, width - sum(sizes)))
    return tuple((sum(sizes[:i]), size) for i, size in enumerate(sizes))


def project(z, a0, a1, gain, weight, rows, first, width, squared):
    depth = a0.shape[1]
    kept = a0.shape[0] // rows // 2
    half = kept * CORES * rows
    tiles = tiles_of(width)
    full = width + (HEAD_DIM if squared else 0)
    vmem = pl.BlockSpec(memory_space=pltpu.VMEM)
    hbm = pl.BlockSpec(memory_space=pltpu.HBM)
    return pl.pallas_call(
        functools.partial(project_kernel, rows, kept, first, tiles, squared),
        out_shape=(
            jax.ShapeDtypeStruct((half, full), f32),
            jax.ShapeDtypeStruct((half, 2 * full - width), bf16),
        ),
        in_specs=[pl.BlockSpec(memory_space=pltpu.SMEM), hbm, hbm, vmem, hbm],
        out_specs=(hbm, vmem),
        scratch_shapes=[
            pltpu.VMEM((2 * half, depth), bf16),
            pltpu.VMEM((2 * half, depth), bf16),
            pltpu.VMEM((depth, width), bf16),
            pltpu.VMEM((half, full), f32),
            pltpu.SemaphoreType.DMA((2 * kept * CORES,)),
            pltpu.SemaphoreType.DMA((len(tiles),)),
            pltpu.SemaphoreType.DMA((len(tiles),)),
        ],
        compiler_params=pltpu.CompilerParams(vmem_limit_bytes=32 * 2**20),
        name="project",
    )(z, a0, a1, gain, weight)


def attend_kernel(plan, rows, per_source, *refs):
    count = len(plan)
    places_ref, lengths_ref, cosine_ref, sine_ref = refs[:4]
    pieces = refs[4 : 4 + count]
    keys_hbm, values_hbm, attended_ref, cache_rows_ref = refs[4 + count : 8 + count]
    keys, values, table, heads, mixed, piece_sems, sems = refs[8 + count :]
    fills = []
    for at, ((source, first, width, start), piece) in enumerate(zip(plan, pieces)):
        fill = pltpu.make_async_copy(
            piece.at[pl.ds(start, rows), :], table.at[places_ref[source], :, pl.ds(first, width)], piece_sems.at[at]
        )
        fill.start()
        fills.append(fill)
    batch = 4
    copies = []
    for at in range(0, rows, batch):
        span = pl.ds(at, batch)
        copies.append(pltpu.make_async_copy(keys_hbm.at[span], keys.at[span], sems.at[0, at // batch]))
        copies.append(pltpu.make_async_copy(values_hbm.at[span], values.at[span], sems.at[1, at // batch]))
    for copy in copies:
        copy.start()
    for fill in fills:
        fill.wait()
    cosine = cosine_ref[...]
    sine = sine_ref[...]
    for h in range(HEADS + 2 * KV_HEADS):
        column = (h % per_source) * HEAD_DIM
        head = table[h // per_source, :, pl.ds(column, HEAD_DIM)].astype(f32)
        if h < HEADS + KV_HEADS:
            head = head * cosine + pltpu.roll(head, HEAD_DIM // 2, 1) * sine
        head = head.astype(bf16)
        if h >= HEADS:
            cache_rows_ref[:, pl.ds((h - HEADS) * HEAD_DIM, HEAD_DIM)] = head
        heads[pl.ds(h * rows, rows), :] = head.astype(f32)
    span = keys.shape[1]
    position = lax.broadcasted_iota(jnp.int32, (HEADS, span), 1)
    for r in range(rows):
        if r % batch == 0:
            copies[r // batch * 2].wait()
            copies[r // batch * 2 + 1].wait()
        query = heads[pl.ds(r, HEADS, stride=rows), :]
        own_key = heads[pl.ds(HEADS * rows + r, KV_HEADS, stride=rows), :]
        own_value = heads[pl.ds((HEADS + KV_HEADS) * rows + r, KV_HEADS, stride=rows), :]
        spread = jnp.concatenate(
            [jnp.broadcast_to(own_key[k : k + 1], (GROUP, HEAD_DIM)) for k in range(KV_HEADS)], axis=0
        )
        own_score = jnp.sum(query * spread, axis=1, keepdims=True) * HEAD_DIM ** (-0.5)
        query = query.astype(bf16)
        scores = jnp.concatenate(
            [
                lax.dot_general(
                    query[k * GROUP : (k + 1) * GROUP],
                    keys[r, :, pl.ds(k * HEAD_DIM, HEAD_DIM)],
                    (((1,), (1,)), ((), ())),
                    preferred_element_type=f32,
                )
                for k in range(KV_HEADS)
            ],
            axis=0,
        ) * HEAD_DIM ** (-0.5)
        masked = jnp.where(position < lengths_ref[r], scores, -jnp.inf)
        top = jnp.maximum(jnp.max(masked, axis=1, keepdims=True), own_score)
        raised = jnp.exp(masked - top)
        raised_own = jnp.exp(own_score - top)
        inverse = 1.0 / (jnp.sum(raised, axis=1, keepdims=True) + raised_own)
        weights = (raised * inverse).astype(bf16)
        own_weight = (raised_own * inverse).astype(bf16).astype(f32)
        result = jnp.concatenate(
            [
                jnp.dot(
                    weights[k * GROUP : (k + 1) * GROUP],
                    values[r, :, pl.ds(k * HEAD_DIM, HEAD_DIM)],
                    preferred_element_type=f32,
                )
                + own_weight[k * GROUP : (k + 1) * GROUP] * own_value[k : k + 1]
                for k in range(KV_HEADS)
            ],
            axis=0,
        )
        mixed[pl.ds(r, HEADS, stride=rows), :] = result
    for h in range(HEADS):
        attended_ref[:, pl.ds(h * HEAD_DIM, HEAD_DIM)] = mixed[pl.ds(h * rows, rows), :].astype(bf16)


def attend(plan, pieces, places, lengths, cosine, sine, key_cache, value_cache, sources, width):
    rows, span, kv_width = key_cache.shape
    smem = pl.BlockSpec(memory_space=pltpu.SMEM)
    vmem = pl.BlockSpec(memory_space=pltpu.VMEM)
    hbm = pl.BlockSpec(memory_space=pltpu.HBM)
    return pl.pallas_call(
        functools.partial(attend_kernel, plan, rows, width // HEAD_DIM),
        out_shape=(
            jax.ShapeDtypeStruct((rows, HEADS * HEAD_DIM), bf16),
            jax.ShapeDtypeStruct((rows, 2 * KV_HEADS * HEAD_DIM), bf16),
        ),
        in_specs=[smem, smem, vmem, vmem] + [hbm] * len(pieces) + [hbm, hbm],
        out_specs=(vmem, vmem),
        scratch_shapes=[
            pltpu.VMEM((rows, span, kv_width), bf16),
            pltpu.VMEM((rows, span, kv_width), bf16),
            pltpu.VMEM((sources, rows, width), bf16),
            pltpu.VMEM(((HEADS + 2 * KV_HEADS) * rows, HEAD_DIM), f32),
            pltpu.VMEM((HEADS * rows, HEAD_DIM), f32),
            pltpu.SemaphoreType.DMA((len(pieces),)),
            pltpu.SemaphoreType.DMA((2, rows // 4)),
        ],
        compiler_params=pltpu.CompilerParams(vmem_limit_bytes=24 * 2**20),
        name="attend",
    )(places, lengths, cosine, sine, *pieces, key_cache, value_cache)


def rotation(lengths):
    half = HEAD_DIM // 2
    steps = jnp.arange(half, dtype=f32)
    inverse = jnp.exp(steps * (-2.0 * math.log(rope_base) / HEAD_DIM))
    angles = lengths.astype(f32)[:, None] * inverse[None, :]
    cosine = jnp.cos(angles)
    sine = jnp.sin(angles)
    return jnp.concatenate([cosine, cosine], axis=1), jnp.concatenate([-sine, sine], axis=1)


def body(hidden_states, norm_gain, projection_weight, key_cache, value_cache, lengths):
    along_x = lax.axis_size("gx")
    along_z = lax.axis_size("gy")
    chips = along_x // CORES
    rows = key_cache.shape[0]
    width = projection_weight.shape[1]
    z = lax.axis_index("gy").reshape(1).astype(jnp.int32)
    gx = lax.axis_index("gx")
    kept = along_z // 2
    first_rows = CORES * rows

    def on_gx(array, shift, flip):
        pairs = [
            ((x + shift) % chips * CORES + (c ^ flip), x * CORES + c)
            for x in range(chips)
            for c in range(CORES)
        ]
        return lax.ppermute(array, "gx", pairs)

    def on_z(array, flip):
        return lax.ppermute(array, "gy", [(s, s ^ flip) for s in range(along_z)])

    def in_hbm(array):
        return pltpu.with_memory_space_constraint(array, pltpu.HBM)

    gain = norm_gain.reshape(1, -1)
    weight = in_hbm(projection_weight)
    there = [on_gx(hidden_states, k, 0) for k in range(1, chips)]
    here = [(in_hbm(hidden_states), on_gx(hidden_states, 0, 1))]
    cosine, sine = rotation(lengths)

    unit = HEAD_DIM * 2
    if width % unit == 0 and width >= 4 * unit:
        cuts = {0: split_at(width, unit, 0.5), 1: split_at(width, unit, 0.6)}
    else:
        cuts = {0: (width,), 1: (width,)}
    plan = []
    pieces = []

    def after(array, other):
        return lax.optimization_barrier((array, other))[0]

    kinds = range(chips)
    chunks = {k: cuts[min(k, 1)] for k in kinds}
    keeps = {k: [] for k in kinds}
    receiveds = {k: [] for k in kinds}
    aways = {}

    def add_pairs(k):
        owns, away = [], []
        for c, chunk in enumerate(chunks[k]):
            keep, received = keeps[k][c], receiveds[k][c]
            if k and c:
                received = after(received, away[2])
            for part, start in ((owns, 0), (away, first_rows)):
                span = slice(start, start + first_rows) if start == 0 else slice(start, None)
                if c == 0:
                    square = (
                        keep[span, :HEAD_DIM]
                        + received[span, :HEAD_DIM].astype(f32)
                        + received[span, HEAD_DIM : 2 * HEAD_DIM].astype(f32)
                    )
                    if start:
                        upper = lax.reduce_precision(square, 8, 7)
                        part.append(upper.astype(bf16))
                        part.append((square - upper).astype(bf16))
                    else:
                        part.append(square)
                skip = HEAD_DIM if c == 0 else 0
                total = keep[span, skip:] + received[span, 2 * skip :].astype(f32)
                part.append(total.astype(bf16) if start else total)
        if k == 0:
            return owns, [jnp.concatenate(away, axis=1)]
        return owns, [jnp.concatenate(away[:3], axis=1), *away[3:]]

    owns = {}
    arrived = {}
    for k in kinds:
        if k:
            a0 = after(there[k - 1], keeps[k - 1])
            a1 = on_gx(a0, 0, 1)
            if len(chunks[0]) > 1:
                a0 = after(a0, receiveds[k - 1][0])
        else:
            a0, a1 = here[0]
        first = 0
        for c, chunk in enumerate(chunks[k]):
            if k == 0 and c:
                a0 = after(a0, keeps[0][0])
            keep, send = project(z, a0, a1, gain, weight, rows, first, chunk, c == 0)
            first += chunk
            keeps[k].append(keep)
            receiveds[k].append(on_z(send, 1))
            if k and c == 0:
                receiveds[k - 1][-1] = after(receiveds[k - 1][-1], keep)
                owns[k - 1], aways[k - 1] = add_pairs(k - 1)
                a0 = after(a0, aways[k - 1])
    owns[chips - 1], aways[chips - 1] = add_pairs(chips - 1)
    for k in kinds:
        arrived[k] = [
            [on_z(away[(i - 1) * first_rows : i * first_rows], 2 * i) for i in range(1, kept)]
            for away in aways[k]
        ]
        if k + 1 < chips:
            arrived[k] = after(arrived[k], keeps[k + 1][-1])
    for k in kinds:
        square = owns[k][0]
        for other in arrived[k][0]:
            square = square + other[:, :HEAD_DIM].astype(f32) + other[:, HEAD_DIM : 2 * HEAD_DIM].astype(f32)
        scale = lax.rsqrt(square[:, :1] * (1.0 / D) + norm_eps)
        done = []
        first = 0
        for c, chunk in enumerate(chunks[k]):
            total = owns[k][c + 1]
            for other in arrived[k][0 if k == 0 else c]:
                skip = 2 * HEAD_DIM + first if k == 0 else (2 * HEAD_DIM if c == 0 else 0)
                total = total + other[:, skip : skip + chunk].astype(f32)
            done.append((total * scale).astype(bf16))
            first += chunk
        first = 0
        for projected in [jnp.concatenate(done, axis=1)] if k == 0 else done:
            if k:
                projected = on_gx(projected, chips - k, 0)
            size = projected.shape[1]
            plan.append((k * CORES, first, size, 0))
            pieces.append(projected)
            plan.append((k * CORES + 1, first, size, rows))
            pieces.append(on_gx(projected, 0, 1))
            first += size
    x, core = gx // CORES, gx % CORES
    places = jnp.stack(
        [
            (x + chips - k) % chips * CORES + jnp.bitwise_xor(core, j)
            for k in range(chips)
            for j in range(CORES)
        ]
    ).astype(jnp.int32)
    return attend(
        plan, pieces, places, lengths, cosine, sine, in_hbm(key_cache), in_hbm(value_cache), along_x, width
    )


def split_at(width, unit, share):
    first = round(width * share / unit) * unit
    return (first, width - first)


def solution(mesh):
    in_specs = (
        P(("groups", "gx"), "gy"),
        P("gy"),
        P("gy", "gx"),
        P(("groups", "gx", "gy"), None, None),
        P(("groups", "gx", "gy"), None, None),
        P(("groups", "gx", "gy")),
    )
    out_specs = (P(("groups", "gx", "gy"), None), P(("groups", "gx", "gy"), None))
    return jax.shard_map(body, mesh=mesh, in_specs=in_specs, out_specs=out_specs, check_vma=False)
```

```python
import functools
import math

import jax
import jax.numpy as jnp
from jax import lax
from jax.experimental import pallas as pl
from jax.experimental.pallas import tpu as pltpu
from jax.sharding import PartitionSpec as P

D = 16384
HEADS = 128
KV_HEADS = 8
HEAD_DIM = 128
GROUP = HEADS // KV_HEADS
CORES = 2
IN_FLIGHT = 3

norm_eps = 1e-05
rope_base = 500000.0
f32 = jnp.float32
bf16 = jnp.bfloat16


def project_kernel(rows, kept, first, tiles, squared, z_ref, a0_ref, a1_ref, gain_ref, w_hbm, keep_hbm, send_ref, raw, acts, w, keep, row_sems, w_sems, keep_sems):
    half = kept * CORES * rows
    loads = []
    for m in range(2 * kept):
        source = pl.multiple_of(jnp.bitwise_xor(z_ref[0], m) * rows, rows)
        for j, ref in enumerate((a0_ref, a1_ref)):
            place = (m % 2) * half + ((m // 2) * CORES + j) * rows
            load = pltpu.make_async_copy(
                ref.at[pl.ds(source, rows), :], raw.at[pl.ds(place, rows), :], row_sems.at[m * CORES + j]
            )
            load.start()
            loads.append((place, load))
    copies = [
        pltpu.make_async_copy(
            w_hbm.at[:, pl.ds(first + begin, width)], w.at[:, pl.ds(begin, width)], w_sems.at[at]
        )
        for at, (begin, width) in enumerate(tiles)
    ]
    for copy in copies[:IN_FLIGHT]:
        copy.start()
    gain = gain_ref[...].astype(f32)
    offset = HEAD_DIM if squared else 0
    for place, load in loads:
        load.wait()
        block = raw[pl.ds(place, rows), :].astype(f32)
        acts[pl.ds(place, rows), :] = (block * gain).astype(bf16)
        if squared:
            square = jnp.broadcast_to(jnp.sum(block * block, axis=1, keepdims=True), (rows, HEAD_DIM))
            if place < half:
                keep[pl.ds(place, rows), pl.ds(0, HEAD_DIM)] = square
            else:
                upper = square.astype(bf16)
                send_ref[pl.ds(place - half, rows), pl.ds(0, HEAD_DIM)] = upper
                lower = (square - upper.astype(f32)).astype(bf16)
                send_ref[pl.ds(place - half, rows), pl.ds(HEAD_DIM, HEAD_DIM)] = lower
    stores = []
    for at, (copy, (begin, width)) in enumerate(zip(copies, tiles)):
        copy.wait()
        if at + IN_FLIGHT < len(copies):
            copies[at + IN_FLIGHT].start()
        total = jnp.dot(acts[...], w[:, pl.ds(begin, width)], preferred_element_type=f32)
        keep[:, pl.ds(offset + begin, width)] = total[:half]
        send_ref[:, pl.ds(2 * offset + begin, width)] = total[half:].astype(bf16)
        left = 0 if at == 0 else offset + begin
        columns = pl.ds(left, offset + begin + width - left)
        store = pltpu.make_async_copy(keep.at[:, columns], keep_hbm.at[:, columns], keep_sems.at[at])
        store.start()
        stores.append(store)
    for store in stores:
        store.wait()


def tiles_of(width):
    sizes = [256] if width % 256 == 0 else []
    while width > sum(sizes):
        sizes.append(min(512, width - sum(sizes)))
    return tuple((sum(sizes[:i]), size) for i, size in enumerate(sizes))


def project(z, a0, a1, gain, weight, rows, first, width, squared):
    depth = a0.shape[1]
    kept = a0.shape[0] // rows // 2
    half = kept * CORES * rows
    tiles = tiles_of(width)
    full = width + (HEAD_DIM if squared else 0)
    vmem = pl.BlockSpec(memory_space=pltpu.VMEM)
    hbm = pl.BlockSpec(memory_space=pltpu.HBM)
    return pl.pallas_call(
        functools.partial(project_kernel, rows, kept, first, tiles, squared),
        out_shape=(
            jax.ShapeDtypeStruct((half, full), f32),
            jax.ShapeDtypeStruct((half, 2 * full - width), bf16),
        ),
        in_specs=[pl.BlockSpec(memory_space=pltpu.SMEM), hbm, hbm, vmem, hbm],
        out_specs=(hbm, vmem),
        scratch_shapes=[
            pltpu.VMEM((2 * half, depth), bf16),
            pltpu.VMEM((2 * half, depth), bf16),
            pltpu.VMEM((depth, width), bf16),
            pltpu.VMEM((half, full), f32),
            pltpu.SemaphoreType.DMA((2 * kept * CORES,)),
            pltpu.SemaphoreType.DMA((len(tiles),)),
            pltpu.SemaphoreType.DMA((len(tiles),)),
        ],
        compiler_params=pltpu.CompilerParams(vmem_limit_bytes=32 * 2**20),
        name="project",
    )(z, a0, a1, gain, weight)


def attend_kernel(plan, rows, per_source, *refs):
    count = len(plan)
    places_ref, lengths_ref, cosine_ref, sine_ref = refs[:4]
    pieces = refs[4 : 4 + count]
    keys, values, _, attended_ref, cache_rows_ref = refs[4 + count : 9 + count]
    heads, scores_ref, weights_ref, mixed = refs[9 + count :]
    cosine = cosine_ref[...]
    sine = sine_ref[...]
    rotated = HEADS + KV_HEADS
    for (source, first, width, start), piece in zip(plan, pieces):
        for column in range(0, width, HEAD_DIM):
            local = (first + column) // HEAD_DIM
            h = places_ref[source] * per_source + local
            head = piece[pl.ds(start, rows), pl.ds(column, HEAD_DIM)].astype(f32)
            turned = head * cosine + pltpu.roll(head, HEAD_DIM // 2, 1) * sine
            if local + KV_HEADS >= per_source:
                turned = jnp.where(h < rotated, turned, head)
            heads[pl.ds(pl.multiple_of(h * rows, rows), rows), :] = turned.astype(bf16).astype(f32)
    for h in range(2 * KV_HEADS):
        cache_rows_ref[:, pl.ds(h * HEAD_DIM, HEAD_DIM)] = heads[pl.ds((HEADS + h) * rows, rows), :].astype(bf16)
    span = keys.shape[1]
    position = lax.broadcasted_iota(jnp.int32, (HEADS, span), 1)

    def score(r):
        query = heads[pl.ds(r, HEADS, stride=rows), :].astype(bf16)
        for k in range(KV_HEADS):
            scores_ref[r, pl.ds(k * GROUP, GROUP), :] = lax.dot_general(
                query[k * GROUP : (k + 1) * GROUP],
                keys[r, :, pl.ds(k * HEAD_DIM, HEAD_DIM)],
                (((1,), (1,)), ((), ())),
                preferred_element_type=f32,
            )

    def soften(r):
        query = heads[pl.ds(r, HEADS, stride=rows), :]
        own_key = heads[pl.ds(HEADS * rows + r, KV_HEADS, stride=rows), :]
        own_value = heads[pl.ds((HEADS + KV_HEADS) * rows + r, KV_HEADS, stride=rows), :]
        spread = jnp.concatenate(
            [jnp.broadcast_to(own_key[k : k + 1], (GROUP, HEAD_DIM)) for k in range(KV_HEADS)], axis=0
        )
        own_score = jnp.sum(query * spread, axis=1, keepdims=True) * HEAD_DIM ** (-0.5)
        masked = jnp.where(position < lengths_ref[r], scores_ref[r] * HEAD_DIM ** (-0.5), -jnp.inf)
        top = jnp.maximum(jnp.max(masked, axis=1, keepdims=True), own_score)
        raised = jnp.exp(masked - top)
        raised_own = jnp.exp(own_score - top)
        inverse = 1.0 / (jnp.sum(raised, axis=1, keepdims=True) + raised_own)
        weights_ref[r] = (raised * inverse).astype(bf16)
        own_weight = (raised_own * inverse).astype(bf16).astype(f32)
        spread = jnp.concatenate(
            [jnp.broadcast_to(own_value[k : k + 1], (GROUP, HEAD_DIM)) for k in range(KV_HEADS)], axis=0
        )
        scores_ref[r] = own_weight * spread

    def mix(r):
        for k in range(KV_HEADS):
            mixed[pl.ds(k * GROUP * rows + r, GROUP, stride=rows), :] = (
                jnp.dot(
                    weights_ref[r, pl.ds(k * GROUP, GROUP), :],
                    values[r, :, pl.ds(k * HEAD_DIM, HEAD_DIM)],
                    preferred_element_type=f32,
                )
                + scores_ref[r, pl.ds(k * GROUP, GROUP), :]
            )

    for r in range(rows):
        score(r)
    for r in range(rows):
        soften(r)
    for r in range(rows):
        mix(r)
    for h in range(HEADS):
        attended_ref[:, pl.ds(h * HEAD_DIM, HEAD_DIM)] = mixed[pl.ds(h * rows, rows), :].astype(bf16)


def attend(plan, pieces, places, lengths, cosine, sine, key_cache, value_cache, fetched, width):
    rows, span, kv_width = key_cache.shape
    smem = pl.BlockSpec(memory_space=pltpu.SMEM)
    vmem = pl.BlockSpec(memory_space=pltpu.VMEM)
    return pl.pallas_call(
        functools.partial(attend_kernel, plan, rows, width // HEAD_DIM),
        out_shape=(
            jax.ShapeDtypeStruct((rows, HEADS * HEAD_DIM), bf16),
            jax.ShapeDtypeStruct((rows, 2 * KV_HEADS * HEAD_DIM), bf16),
        ),
        in_specs=[smem, smem] + [vmem] * (len(pieces) + 5),
        out_specs=(vmem, vmem),
        scratch_shapes=[
            pltpu.VMEM(((HEADS + 2 * KV_HEADS) * rows, HEAD_DIM), f32),
            pltpu.VMEM((rows, HEADS, span), f32),
            pltpu.VMEM((rows, HEADS, span), bf16),
            pltpu.VMEM((HEADS * rows, HEAD_DIM), f32),
        ],
        compiler_params=pltpu.CompilerParams(vmem_limit_bytes=12 * 2**20),
        name="attend",
    )(places, lengths, cosine, sine, *pieces, key_cache, value_cache, fetched)


def fetch_kernel(keys_hbm, values_hbm, keys, values, fetched, sems):
    loads = [
        pltpu.make_async_copy(keys_hbm, keys, sems.at[0]),
        pltpu.make_async_copy(values_hbm, values, sems.at[1]),
    ]
    for load in loads:
        load.start()
    for load in loads:
        load.wait()
    fetched[...] = jnp.zeros_like(fetched)


def fetch(key_cache, value_cache):
    vmem = pl.BlockSpec(memory_space=pltpu.VMEM)
    hbm = pl.BlockSpec(memory_space=pltpu.HBM)
    shape = jax.ShapeDtypeStruct(key_cache.shape, bf16)
    return pl.pallas_call(
        fetch_kernel,
        out_shape=(shape, shape, jax.ShapeDtypeStruct((8, 128), f32)),
        in_specs=[hbm, hbm],
        out_specs=(vmem, vmem, vmem),
        scratch_shapes=[pltpu.SemaphoreType.DMA((2,))],
        compiler_params=pltpu.CompilerParams(vmem_limit_bytes=16 * 2**20),
        name="fetch",
    )(key_cache, value_cache)


def rotation(lengths):
    half = HEAD_DIM // 2
    steps = jnp.arange(half, dtype=f32)
    inverse = jnp.exp(steps * (-2.0 * math.log(rope_base) / HEAD_DIM))
    angles = lengths.astype(f32)[:, None] * inverse[None, :]
    cosine = jnp.cos(angles)
    sine = jnp.sin(angles)
    return jnp.concatenate([cosine, cosine], axis=1), jnp.concatenate([-sine, sine], axis=1)


def body(hidden_states, norm_gain, projection_weight, key_cache, value_cache, lengths):
    along_x = lax.axis_size("gx")
    along_z = lax.axis_size("gy")
    chips = along_x // CORES
    rows = key_cache.shape[0]
    width = projection_weight.shape[1]
    z = lax.axis_index("gy").reshape(1).astype(jnp.int32)
    gx = lax.axis_index("gx")
    kept = along_z // 2
    first_rows = CORES * rows

    def on_gx(array, shift, flip):
        pairs = [
            ((x + shift) % chips * CORES + (c ^ flip), x * CORES + c)
            for x in range(chips)
            for c in range(CORES)
        ]
        return lax.ppermute(array, "gx", pairs)

    def on_z(array, flip):
        return lax.ppermute(array, "gy", [(s, s ^ flip) for s in range(along_z)])

    def in_hbm(array):
        return pltpu.with_memory_space_constraint(array, pltpu.HBM)

    gain = norm_gain.reshape(1, -1)
    weight = in_hbm(projection_weight)
    there = [on_gx(hidden_states, k, 0) for k in range(1, chips)]
    here = [(in_hbm(hidden_states), on_gx(hidden_states, 0, 1))]
    cosine, sine = rotation(lengths)

    unit = HEAD_DIM * 2
    if width % unit == 0 and width >= 4 * unit:
        cuts = {0: split_at(width, unit, 0.5), 1: split_at(width, unit, 0.6)}
    else:
        cuts = {0: (width,), 1: (width,)}
    plan = []
    pieces = []

    def after(array, other):
        return lax.optimization_barrier((array, other))[0]

    kinds = range(chips)
    chunks = {k: cuts[min(k, 1)] for k in kinds}
    keeps = {k: [] for k in kinds}
    receiveds = {k: [] for k in kinds}
    aways = {}

    def add_pairs(k):
        owns, away = [], []
        for c, chunk in enumerate(chunks[k]):
            keep, received = keeps[k][c], receiveds[k][c]
            if k and c:
                received = after(received, away[2])
            for part, start in ((owns, 0), (away, first_rows)):
                span = slice(start, start + first_rows) if start == 0 else slice(start, None)
                if c == 0:
                    square = (
                        keep[span, :HEAD_DIM]
                        + received[span, :HEAD_DIM].astype(f32)
                        + received[span, HEAD_DIM : 2 * HEAD_DIM].astype(f32)
                    )
                    if start:
                        upper = lax.reduce_precision(square, 8, 7)
                        part.append(upper.astype(bf16))
                        part.append((square - upper).astype(bf16))
                    else:
                        part.append(square)
                skip = HEAD_DIM if c == 0 else 0
                total = keep[span, skip:] + received[span, 2 * skip :].astype(f32)
                part.append(total.astype(bf16) if start else total)
        if k == 0:
            return owns, [jnp.concatenate(away, axis=1)]
        return owns, [jnp.concatenate(away[:3], axis=1), *away[3:]]

    owns = {}
    arrived = {}
    for k in kinds:
        if k:
            a0 = after(there[k - 1], keeps[k - 1])
            a1 = on_gx(a0, 0, 1)
            if len(chunks[0]) > 1:
                a0 = after(a0, receiveds[k - 1][0])
        else:
            a0, a1 = here[0]
        first = 0
        for c, chunk in enumerate(chunks[k]):
            if k == 0 and c:
                a0 = after(a0, keeps[0][0])
            keep, send = project(z, a0, a1, gain, weight, rows, first, chunk, c == 0)
            first += chunk
            keeps[k].append(keep)
            receiveds[k].append(on_z(send, 1))
            if k and c == 0:
                receiveds[k - 1][-1] = after(receiveds[k - 1][-1], keep)
                owns[k - 1], aways[k - 1] = add_pairs(k - 1)
                a0 = after(a0, aways[k - 1])
    owns[chips - 1], aways[chips - 1] = add_pairs(chips - 1)
    for k in kinds:
        arrived[k] = [
            [on_z(away[(i - 1) * first_rows : i * first_rows], 2 * i) for i in range(1, kept)]
            for away in aways[k]
        ]
        if k + 1 < chips:
            arrived[k] = after(arrived[k], keeps[k + 1][-1])
    for k in kinds:
        square = owns[k][0]
        for other in arrived[k][0]:
            square = square + other[:, :HEAD_DIM].astype(f32) + other[:, HEAD_DIM : 2 * HEAD_DIM].astype(f32)
        scale = lax.rsqrt(square[:, :1] * (1.0 / D) + norm_eps)
        done = []
        first = 0
        for c, chunk in enumerate(chunks[k]):
            total = owns[k][c + 1]
            for other in arrived[k][0 if k == 0 else c]:
                skip = 2 * HEAD_DIM + first if k == 0 else (2 * HEAD_DIM if c == 0 else 0)
                total = total + other[:, skip : skip + chunk].astype(f32)
            done.append((total * scale).astype(bf16))
            first += chunk
        first = 0
        sent = [jnp.concatenate(done, axis=1)] if k == 0 else [on_gx(part, chips - k, 0) for part in done]
        if k + 1 == chips:
            keys, values, fetched = fetch(in_hbm(after(key_cache, done)), in_hbm(value_cache))
            sent, fetched = lax.optimization_barrier((sent, fetched))
        for projected in sent:
            size = projected.shape[1]
            plan.append((k * CORES, first, size, 0))
            pieces.append(projected)
            plan.append((k * CORES + 1, first, size, rows))
            pieces.append(on_gx(projected, 0, 1))
            first += size
    x, core = gx // CORES, gx % CORES
    places = jnp.stack(
        [
            (x + chips - k) % chips * CORES + jnp.bitwise_xor(core, j)
            for k in range(chips)
            for j in range(CORES)
        ]
    ).astype(jnp.int32)
    return attend(
        plan, pieces, places, lengths, cosine, sine, keys, values, fetched, width
    )


def split_at(width, unit, share):
    first = round(width * share / unit) * unit
    return (first, width - first)


def solution(mesh):
    in_specs = (
        P(("groups", "gx"), "gy"),
        P("gy"),
        P("gy", "gx"),
        P(("groups", "gx", "gy"), None, None),
        P(("groups", "gx", "gy"), None, None),
        P(("groups", "gx", "gy")),
    )
    out_specs = (P(("groups", "gx", "gy"), None), P(("groups", "gx", "gy"), None))
    return jax.shard_map(body, mesh=mesh, in_specs=in_specs, out_specs=out_specs, check_vma=False)
```

```python
import functools
import math

import jax
import jax.numpy as jnp
from jax import lax
from jax.experimental import pallas as pl
from jax.experimental.pallas import tpu as pltpu
from jax.sharding import PartitionSpec as P

D = 16384
HEADS = 128
KV_HEADS = 8
HEAD_DIM = 128
GROUP = HEADS // KV_HEADS
CORES = 2
IN_FLIGHT = 3

norm_eps = 1e-05
rope_base = 500000.0
f32 = jnp.float32
bf16 = jnp.bfloat16


def project_kernel(rows, kept, first, tiles, squared, z_ref, a0_ref, a1_ref, gain_ref, w_hbm, keep_hbm, send_ref, raw, acts, w, keep, row_sems, w_sems, keep_sems):
    half = kept * CORES * rows
    loads = []
    for m in range(2 * kept):
        source = pl.multiple_of(jnp.bitwise_xor(z_ref[0], m) * rows, rows)
        for j, ref in enumerate((a0_ref, a1_ref)):
            place = (m % 2) * half + ((m // 2) * CORES + j) * rows
            load = pltpu.make_async_copy(
                ref.at[pl.ds(source, rows), :], raw.at[pl.ds(place, rows), :], row_sems.at[m * CORES + j]
            )
            load.start()
            loads.append((place, load))
    copies = [
        pltpu.make_async_copy(
            w_hbm.at[:, pl.ds(first + begin, width)], w.at[:, pl.ds(begin, width)], w_sems.at[at]
        )
        for at, (begin, width) in enumerate(tiles)
    ]
    for copy in copies[:IN_FLIGHT]:
        copy.start()
    gain = gain_ref[...].astype(f32)
    offset = HEAD_DIM if squared else 0
    for place, load in loads:
        load.wait()
        block = raw[pl.ds(place, rows), :].astype(f32)
        acts[pl.ds(place, rows), :] = (block * gain).astype(bf16)
        if squared:
            square = jnp.broadcast_to(jnp.sum(block * block, axis=1, keepdims=True), (rows, HEAD_DIM))
            if place < half:
                keep[pl.ds(place, rows), pl.ds(0, HEAD_DIM)] = square
            else:
                upper = square.astype(bf16)
                send_ref[pl.ds(place - half, rows), pl.ds(0, HEAD_DIM)] = upper
                lower = (square - upper.astype(f32)).astype(bf16)
                send_ref[pl.ds(place - half, rows), pl.ds(HEAD_DIM, HEAD_DIM)] = lower
    stores = []
    for at, (copy, (begin, width)) in enumerate(zip(copies, tiles)):
        copy.wait()
        if at + IN_FLIGHT < len(copies):
            copies[at + IN_FLIGHT].start()
        total = jnp.dot(acts[...], w[:, pl.ds(begin, width)], preferred_element_type=f32)
        keep[:, pl.ds(offset + begin, width)] = total[:half]
        send_ref[:, pl.ds(2 * offset + begin, width)] = total[half:].astype(bf16)
        left = 0 if at == 0 else offset + begin
        columns = pl.ds(left, offset + begin + width - left)
        store = pltpu.make_async_copy(keep.at[:, columns], keep_hbm.at[:, columns], keep_sems.at[at])
        store.start()
        stores.append(store)
    for store in stores:
        store.wait()


def tiles_of(width):
    sizes = [256] if width % 256 == 0 else []
    while width > sum(sizes):
        sizes.append(min(512, width - sum(sizes)))
    return tuple((sum(sizes[:i]), size) for i, size in enumerate(sizes))


def project(z, a0, a1, gain, weight, rows, first, width, squared):
    depth = a0.shape[1]
    kept = a0.shape[0] // rows // 2
    half = kept * CORES * rows
    tiles = tiles_of(width)
    full = width + (HEAD_DIM if squared else 0)
    vmem = pl.BlockSpec(memory_space=pltpu.VMEM)
    hbm = pl.BlockSpec(memory_space=pltpu.HBM)
    return pl.pallas_call(
        functools.partial(project_kernel, rows, kept, first, tiles, squared),
        out_shape=(
            jax.ShapeDtypeStruct((half, full), f32),
            jax.ShapeDtypeStruct((half, 2 * full - width), bf16),
        ),
        in_specs=[pl.BlockSpec(memory_space=pltpu.SMEM), hbm, hbm, vmem, hbm],
        out_specs=(hbm, vmem),
        scratch_shapes=[
            pltpu.VMEM((2 * half, depth), bf16),
            pltpu.VMEM((2 * half, depth), bf16),
            pltpu.VMEM((depth, width), bf16),
            pltpu.VMEM((half, full), f32),
            pltpu.SemaphoreType.DMA((2 * kept * CORES,)),
            pltpu.SemaphoreType.DMA((len(tiles),)),
            pltpu.SemaphoreType.DMA((len(tiles),)),
        ],
        compiler_params=pltpu.CompilerParams(vmem_limit_bytes=32 * 2**20),
        name="project",
    )(z, a0, a1, gain, weight)


def attend_kernel(plan, rows, per_source, *refs):
    count = len(plan)
    places_ref, lengths_ref, cosine_ref, sine_ref = refs[:4]
    pieces = refs[4 : 4 + count]
    keys, values, _, attended_ref, cache_rows_ref = refs[4 + count : 9 + count]
    heads, scores_ref, weights_ref, mixed = refs[9 + count :]
    cosine = cosine_ref[...]
    sine = sine_ref[...]
    rotated = HEADS + KV_HEADS
    for (source, first, width, start), piece in zip(plan, pieces):
        for column in range(0, width, HEAD_DIM):
            local = (first + column) // HEAD_DIM
            h = places_ref[source] * per_source + local
            head = piece[pl.ds(start, rows), pl.ds(column, HEAD_DIM)].astype(f32)
            turned = head * cosine + pltpu.roll(head, HEAD_DIM // 2, 1) * sine
            if local + KV_HEADS >= per_source:
                turned = jnp.where(h < rotated, turned, head)
            heads[pl.ds(pl.multiple_of(h * rows, rows), rows), :] = turned.astype(bf16).astype(f32)
    for h in range(2 * KV_HEADS):
        cache_rows_ref[:, pl.ds(h * HEAD_DIM, HEAD_DIM)] = heads[pl.ds((HEADS + h) * rows, rows), :].astype(bf16)
    span = keys.shape[1]
    position = lax.broadcasted_iota(jnp.int32, (HEADS, span), 1)

    def score(r):
        query = heads[pl.ds(r, HEADS, stride=rows), :].astype(bf16)
        for k in range(KV_HEADS):
            scores_ref[r, pl.ds(k * GROUP, GROUP), :] = lax.dot_general(
                query[k * GROUP : (k + 1) * GROUP],
                keys[r, :, pl.ds(k * HEAD_DIM, HEAD_DIM)],
                (((1,), (1,)), ((), ())),
                preferred_element_type=f32,
            )

    def soften(r):
        query = heads[pl.ds(r, HEADS, stride=rows), :]
        own_key = heads[pl.ds(HEADS * rows + r, KV_HEADS, stride=rows), :]
        own_value = heads[pl.ds((HEADS + KV_HEADS) * rows + r, KV_HEADS, stride=rows), :]
        spread = jnp.concatenate(
            [jnp.broadcast_to(own_key[k : k + 1], (GROUP, HEAD_DIM)) for k in range(KV_HEADS)], axis=0
        )
        own_score = jnp.sum(query * spread, axis=1, keepdims=True) * HEAD_DIM ** (-0.5)
        masked = jnp.where(position < lengths_ref[r], scores_ref[r] * HEAD_DIM ** (-0.5), -jnp.inf)
        top = jnp.maximum(jnp.max(masked, axis=1, keepdims=True), own_score)
        raised = jnp.exp(masked - top)
        raised_own = jnp.exp(own_score - top)
        inverse = 1.0 / (jnp.sum(raised, axis=1, keepdims=True) + raised_own)
        weights_ref[r] = (raised * inverse).astype(bf16)
        own_weight = (raised_own * inverse).astype(bf16).astype(f32)
        spread = jnp.concatenate(
            [jnp.broadcast_to(own_value[k : k + 1], (GROUP, HEAD_DIM)) for k in range(KV_HEADS)], axis=0
        )
        scores_ref[r] = own_weight * spread

    def mix(r):
        for k in range(KV_HEADS):
            mixed[pl.ds(k * GROUP * rows + r, GROUP, stride=rows), :] = (
                jnp.dot(
                    weights_ref[r, pl.ds(k * GROUP, GROUP), :],
                    values[r, :, pl.ds(k * HEAD_DIM, HEAD_DIM)],
                    preferred_element_type=f32,
                )
                + scores_ref[r, pl.ds(k * GROUP, GROUP), :]
            )

    for r in range(rows):
        score(r)
    for r in range(rows):
        soften(r)
    for r in range(rows):
        mix(r)
    for h in range(HEADS):
        attended_ref[:, pl.ds(h * HEAD_DIM, HEAD_DIM)] = mixed[pl.ds(h * rows, rows), :].astype(bf16)


def attend(plan, pieces, places, lengths, cosine, sine, key_cache, value_cache, fetched, width):
    rows, span, kv_width = key_cache.shape
    smem = pl.BlockSpec(memory_space=pltpu.SMEM)
    vmem = pl.BlockSpec(memory_space=pltpu.VMEM)
    return pl.pallas_call(
        functools.partial(attend_kernel, plan, rows, width // HEAD_DIM),
        out_shape=(
            jax.ShapeDtypeStruct((rows, HEADS * HEAD_DIM), bf16),
            jax.ShapeDtypeStruct((rows, 2 * KV_HEADS * HEAD_DIM), bf16),
        ),
        in_specs=[smem, smem] + [vmem] * (len(pieces) + 5),
        out_specs=(vmem, vmem),
        scratch_shapes=[
            pltpu.VMEM(((HEADS + 2 * KV_HEADS) * rows, HEAD_DIM), f32),
            pltpu.VMEM((rows, HEADS, span), f32),
            pltpu.VMEM((rows, HEADS, span), bf16),
            pltpu.VMEM((HEADS * rows, HEAD_DIM), f32),
        ],
        compiler_params=pltpu.CompilerParams(vmem_limit_bytes=12 * 2**20),
        name="attend",
    )(places, lengths, cosine, sine, *pieces, key_cache, value_cache, fetched)


def fetch_kernel(keys_hbm, values_hbm, keys, values, fetched, sems):
    loads = [
        pltpu.make_async_copy(keys_hbm, keys, sems.at[0]),
        pltpu.make_async_copy(values_hbm, values, sems.at[1]),
    ]
    for load in loads:
        load.start()
    for load in loads:
        load.wait()
    fetched[...] = jnp.zeros_like(fetched)


def fetch(key_cache, value_cache):
    vmem = pl.BlockSpec(memory_space=pltpu.VMEM)
    hbm = pl.BlockSpec(memory_space=pltpu.HBM)
    shape = jax.ShapeDtypeStruct(key_cache.shape, bf16)
    return pl.pallas_call(
        fetch_kernel,
        out_shape=(shape, shape, jax.ShapeDtypeStruct((8, 128), f32)),
        in_specs=[hbm, hbm],
        out_specs=(vmem, vmem, vmem),
        scratch_shapes=[pltpu.SemaphoreType.DMA((2,))],
        compiler_params=pltpu.CompilerParams(vmem_limit_bytes=16 * 2**20),
        name="fetch",
    )(key_cache, value_cache)


def rotation(lengths):
    half = HEAD_DIM // 2
    steps = jnp.arange(half, dtype=f32)
    inverse = jnp.exp(steps * (-2.0 * math.log(rope_base) / HEAD_DIM))
    angles = lengths.astype(f32)[:, None] * inverse[None, :]
    cosine = jnp.cos(angles)
    sine = jnp.sin(angles)
    return jnp.concatenate([cosine, cosine], axis=1), jnp.concatenate([-sine, sine], axis=1)


def body(hidden_states, norm_gain, projection_weight, key_cache, value_cache, lengths):
    along_x = lax.axis_size("gx")
    along_z = lax.axis_size("gy")
    chips = along_x // CORES
    rows = key_cache.shape[0]
    width = projection_weight.shape[1]
    z = lax.axis_index("gy").reshape(1).astype(jnp.int32)
    gx = lax.axis_index("gx")
    kept = along_z // 2
    first_rows = CORES * rows

    def on_gx(array, shift, flip):
        pairs = [
            ((x + shift) % chips * CORES + (c ^ flip), x * CORES + c)
            for x in range(chips)
            for c in range(CORES)
        ]
        return lax.ppermute(array, "gx", pairs)

    def on_z(array, flip):
        return lax.ppermute(array, "gy", [(s, s ^ flip) for s in range(along_z)])

    def in_hbm(array):
        return pltpu.with_memory_space_constraint(array, pltpu.HBM)

    gain = norm_gain.reshape(1, -1)
    weight = in_hbm(projection_weight)
    there = [on_gx(hidden_states, k, 0) for k in range(1, chips)]
    here = [(in_hbm(hidden_states), on_gx(hidden_states, 0, 1))]
    cosine, sine = rotation(lengths)

    unit = HEAD_DIM * 2
    if width % unit == 0 and width >= 4 * unit:
        cuts = {0: split_at(width, unit, 0.5), 1: split_at(width, unit, 0.6)}
    else:
        cuts = {0: (width,), 1: (width,)}
    plan = []
    pieces = []

    def tie(*arrays):
        return lax.optimization_barrier(arrays)

    units = [
        (k, sum(cuts[min(k, 1)][:c]), chunk, c == 0)
        for k in range(chips)
        for c, chunk in enumerate(cuts[min(k, 1)])
    ]
    count = len(units)
    keeps, receiveds, owns, aways, arrived = [], [], [], [], []

    def add_pair(keep, received, squared):
        results = []
        for rest in (False, True):
            span = slice(first_rows, None) if rest else slice(0, first_rows)
            skip = HEAD_DIM if squared else 0
            parts = []
            if squared:
                square = (
                    keep[span, :HEAD_DIM]
                    + received[span, :HEAD_DIM].astype(f32)
                    + received[span, HEAD_DIM : 2 * HEAD_DIM].astype(f32)
                )
                upper = lax.reduce_precision(square, 8, 7)
                parts = [upper.astype(bf16), (square - upper).astype(bf16)] if rest else [square]
            total = keep[span, skip:] + received[span, 2 * skip :].astype(f32)
            results.append(parts + [total.astype(bf16) if rest else total])
        return results

    def step_one(u):
        own, away = add_pair(keeps[u], receiveds[u], units[u][3])
        owns.append(own)
        aways.append(jnp.concatenate(away, axis=1) if len(away) > 1 else away[0])

    def step_two(u):
        away = aways[u]
        arrived.append([on_z(away[(i - 1) * first_rows : i * first_rows], 2 * i) for i in range(1, kept)])

    for u, (k, first, chunk, squared) in enumerate(units):
        if u > 1:
            receiveds[u - 2], keeps[u - 1] = tie(receiveds[u - 2], keeps[u - 1])
        if squared and k:
            array, keeps[u - 1] = tie(there[k - 1], keeps[u - 1])
            a0, a1 = array, on_gx(array, 0, 1)
        elif squared:
            a0, a1 = here[0]
        else:
            a0, keeps[u - 1] = tie(a0, keeps[u - 1])
        if u > 1:
            step_one(u - 2)
            a0, aways[u - 2] = tie(a0, aways[u - 2])
            step_two(u - 2)
        if u > 2:
            a0, arrived[u - 3] = tie(a0, arrived[u - 3])
        keep, send = project(z, a0, a1, gain, weight, rows, first, chunk, squared)
        keeps.append(keep)
        receiveds.append(on_z(send, 1))
    plan, pieces, scales, projecteds = [], [], {}, []

    def finish(u):
        k, first, chunk, squared = units[u]
        own, others = owns[u], arrived[u]
        skip = 2 * HEAD_DIM if squared else 0
        if squared:
            square = own[0]
            for other in others:
                square = square + other[:, :HEAD_DIM].astype(f32) + other[:, HEAD_DIM:skip].astype(f32)
            scales[k] = lax.rsqrt(square[:, :1] * (1.0 / D) + norm_eps)
        total = own[-1]
        for other in others:
            total = total + other[:, skip:].astype(f32)
        projecteds.append((total * scales[k]).astype(bf16))

    def hand_out(u):
        k, first, chunk, squared = units[u]
        projected = projecteds[u]
        if k:
            projected = on_gx(projected, chips - k, 0)
        plan.append((k * CORES, first, chunk, 0))
        plan.append((k * CORES + 1, first, chunk, rows))
        return projected

    for u in range(max(count - 2, 0), count):
        if u + 1 < count and u:
            receiveds[u], keeps[u + 1], arrived[u - 1] = tie(receiveds[u], keeps[u + 1], arrived[u - 1])
        elif u:
            *arrived[:], aways[u - 1] = tie(*arrived, aways[u - 1])
            step_two(u - 1)
            for before in range(u - 1):
                finish(before)
            if projecteds:
                receiveds[u], projecteds[-1], aways[u - 1] = tie(receiveds[u], projecteds[-1], aways[u - 1])
        step_one(u)
    step_two(count - 1)
    if count > 1:
        finish(count - 2)
    finish(count - 1)
    projecteds[-1], key_cache = tie(projecteds[-1], key_cache)
    keys, values, fetched = fetch(in_hbm(key_cache), in_hbm(value_cache))
    held = [hand_out(u) for u in range(count)]
    held[-1], fetched = tie(held[-1], fetched)
    for projected in held:
        pieces.append(projected)
        pieces.append(on_gx(projected, 0, 1))
    x, core = gx // CORES, gx % CORES
    places = jnp.stack(
        [
            (x + chips - k) % chips * CORES + jnp.bitwise_xor(core, j)
            for k in range(chips)
            for j in range(CORES)
        ]
    ).astype(jnp.int32)
    return attend(
        plan, pieces, places, lengths, cosine, sine, keys, values, fetched, width
    )


def split_at(width, unit, share):
    first = round(width * share / unit) * unit
    return (first, width - first)


def solution(mesh):
    in_specs = (
        P(("groups", "gx"), "gy"),
        P("gy"),
        P("gy", "gx"),
        P(("groups", "gx", "gy"), None, None),
        P(("groups", "gx", "gy"), None, None),
        P(("groups", "gx", "gy")),
    )
    out_specs = (P(("groups", "gx", "gy"), None), P(("groups", "gx", "gy"), None))
    return jax.shard_map(body, mesh=mesh, in_specs=in_specs, out_specs=out_specs, check_vma=False)
```

```python
import functools
import math

import jax
import jax.numpy as jnp
from jax import lax
from jax.experimental import pallas as pl
from jax.experimental.pallas import tpu as pltpu
from jax.sharding import PartitionSpec as P

D = 16384
HEADS = 128
KV_HEADS = 8
HEAD_DIM = 128
GROUP = HEADS // KV_HEADS
CORES = 2
IN_FLIGHT = 3
OWN_SHARE = 2 / 3
OTHER_SHARE = 0.5

norm_eps = 1e-05
rope_base = 500000.0
f32 = jnp.float32
bf16 = jnp.bfloat16


def project_kernel(rows, kept, first, tiles, squared, z_ref, a0_ref, a1_ref, gain_ref, w_hbm, keep_hbm, send_ref, raw, acts, w, keep, row_sems, w_sems, keep_sems):
    half = kept * CORES * rows
    loads = []
    for m in range(2 * kept):
        source = pl.multiple_of(jnp.bitwise_xor(z_ref[0], m) * rows, rows)
        for j, ref in enumerate((a0_ref, a1_ref)):
            place = (m % 2) * half + ((m // 2) * CORES + j) * rows
            load = pltpu.make_async_copy(
                ref.at[pl.ds(source, rows), :], raw.at[pl.ds(place, rows), :], row_sems.at[m * CORES + j]
            )
            load.start()
            loads.append((place, load))
    copies = [
        pltpu.make_async_copy(
            w_hbm.at[:, pl.ds(first + begin, width)], w.at[:, pl.ds(begin, width)], w_sems.at[at]
        )
        for at, (begin, width) in enumerate(tiles)
    ]
    for copy in copies[:IN_FLIGHT]:
        copy.start()
    gain = gain_ref[...].astype(f32)
    offset = HEAD_DIM if squared else 0
    for place, load in loads:
        load.wait()
        block = raw[pl.ds(place, rows), :].astype(f32)
        acts[pl.ds(place, rows), :] = (block * gain).astype(bf16)
        if squared:
            square = jnp.broadcast_to(jnp.sum(block * block, axis=1, keepdims=True), (rows, HEAD_DIM))
            if place < half:
                keep[pl.ds(place, rows), pl.ds(0, HEAD_DIM)] = square
            else:
                upper = square.astype(bf16)
                send_ref[pl.ds(place - half, rows), pl.ds(0, HEAD_DIM)] = upper
                lower = (square - upper.astype(f32)).astype(bf16)
                send_ref[pl.ds(place - half, rows), pl.ds(HEAD_DIM, HEAD_DIM)] = lower
    stores = []
    for at, (copy, (begin, width)) in enumerate(zip(copies, tiles)):
        copy.wait()
        if at + IN_FLIGHT < len(copies):
            copies[at + IN_FLIGHT].start()
        total = jnp.dot(acts[...], w[:, pl.ds(begin, width)], preferred_element_type=f32)
        keep[:, pl.ds(offset + begin, width)] = total[:half]
        send_ref[:, pl.ds(2 * offset + begin, width)] = total[half:].astype(bf16)
        left = 0 if at == 0 else offset + begin
        columns = pl.ds(left, offset + begin + width - left)
        store = pltpu.make_async_copy(keep.at[:, columns], keep_hbm.at[:, columns], keep_sems.at[at])
        store.start()
        stores.append(store)
    for store in stores:
        store.wait()


def tiles_of(width):
    sizes = [256] if width % 256 == 0 else []
    while width > sum(sizes):
        sizes.append(min(512, width - sum(sizes)))
    return tuple((sum(sizes[:i]), size) for i, size in enumerate(sizes))


def project(z, a0, a1, gain, weight, rows, first, width, squared):
    depth = a0.shape[1]
    kept = a0.shape[0] // rows // 2
    half = kept * CORES * rows
    tiles = tiles_of(width)
    full = width + (HEAD_DIM if squared else 0)
    vmem = pl.BlockSpec(memory_space=pltpu.VMEM)
    hbm = pl.BlockSpec(memory_space=pltpu.HBM)
    return pl.pallas_call(
        functools.partial(project_kernel, rows, kept, first, tiles, squared),
        out_shape=(
            jax.ShapeDtypeStruct((half, full), f32),
            jax.ShapeDtypeStruct((half, 2 * full - width), bf16),
        ),
        in_specs=[pl.BlockSpec(memory_space=pltpu.SMEM), hbm, hbm, vmem, hbm],
        out_specs=(hbm, vmem),
        scratch_shapes=[
            pltpu.VMEM((2 * half, depth), bf16),
            pltpu.VMEM((2 * half, depth), bf16),
            pltpu.VMEM((depth, width), bf16),
            pltpu.VMEM((half, full), f32),
            pltpu.SemaphoreType.DMA((2 * kept * CORES,)),
            pltpu.SemaphoreType.DMA((len(tiles),)),
            pltpu.SemaphoreType.DMA((len(tiles),)),
        ],
        compiler_params=pltpu.CompilerParams(vmem_limit_bytes=32 * 2**20),
        name="project",
    )(z, a0, a1, gain, weight)


def attend_kernel(plan, rows, per_source, *refs):
    count = len(plan)
    places_ref, lengths_ref, cosine_ref, sine_ref = refs[:4]
    pieces = refs[4 : 4 + count]
    keys, values, _, attended_ref, cache_rows_ref = refs[4 + count : 9 + count]
    heads, scores_ref, weights_ref, mixed = refs[9 + count :]
    cosine = cosine_ref[...]
    sine = sine_ref[...]
    rotated = HEADS + KV_HEADS
    for (source, first, width, start), piece in zip(plan, pieces):
        for column in range(0, width, HEAD_DIM):
            local = (first + column) // HEAD_DIM
            h = places_ref[source] * per_source + local
            head = piece[pl.ds(start, rows), pl.ds(column, HEAD_DIM)].astype(f32)
            turned = head * cosine + pltpu.roll(head, HEAD_DIM // 2, 1) * sine
            if local + KV_HEADS >= per_source:
                turned = jnp.where(h < rotated, turned, head)
            heads[pl.ds(pl.multiple_of(h * rows, rows), rows), :] = turned.astype(bf16).astype(f32)
    for h in range(2 * KV_HEADS):
        cache_rows_ref[:, pl.ds(h * HEAD_DIM, HEAD_DIM)] = heads[pl.ds((HEADS + h) * rows, rows), :].astype(bf16)
    span = keys.shape[1]
    position = lax.broadcasted_iota(jnp.int32, (HEADS, span), 1)

    def score(r):
        query = heads[pl.ds(r, HEADS, stride=rows), :].astype(bf16)
        for k in range(KV_HEADS):
            scores_ref[r, pl.ds(k * GROUP, GROUP), :] = lax.dot_general(
                query[k * GROUP : (k + 1) * GROUP],
                keys[r, :, pl.ds(k * HEAD_DIM, HEAD_DIM)],
                (((1,), (1,)), ((), ())),
                preferred_element_type=f32,
            )

    def soften(r):
        query = heads[pl.ds(r, HEADS, stride=rows), :]
        own_key = heads[pl.ds(HEADS * rows + r, KV_HEADS, stride=rows), :]
        own_value = heads[pl.ds((HEADS + KV_HEADS) * rows + r, KV_HEADS, stride=rows), :]
        spread = jnp.concatenate(
            [jnp.broadcast_to(own_key[k : k + 1], (GROUP, HEAD_DIM)) for k in range(KV_HEADS)], axis=0
        )
        own_score = jnp.sum(query * spread, axis=1, keepdims=True) * HEAD_DIM ** (-0.5)
        masked = jnp.where(position < lengths_ref[r], scores_ref[r] * HEAD_DIM ** (-0.5), -jnp.inf)
        top = jnp.maximum(jnp.max(masked, axis=1, keepdims=True), own_score)
        raised = jnp.exp(masked - top)
        raised_own = jnp.exp(own_score - top)
        inverse = 1.0 / (jnp.sum(raised, axis=1, keepdims=True) + raised_own)
        weights_ref[r] = (raised * inverse).astype(bf16)
        own_weight = (raised_own * inverse).astype(bf16).astype(f32)
        spread = jnp.concatenate(
            [jnp.broadcast_to(own_value[k : k + 1], (GROUP, HEAD_DIM)) for k in range(KV_HEADS)], axis=0
        )
        scores_ref[r] = own_weight * spread

    def mix(r):
        for k in range(KV_HEADS):
            mixed[pl.ds(k * GROUP * rows + r, GROUP, stride=rows), :] = (
                jnp.dot(
                    weights_ref[r, pl.ds(k * GROUP, GROUP), :],
                    values[r, :, pl.ds(k * HEAD_DIM, HEAD_DIM)],
                    preferred_element_type=f32,
                )
                + scores_ref[r, pl.ds(k * GROUP, GROUP), :]
            )

    for r in range(rows):
        score(r)
    for r in range(rows):
        soften(r)
    for r in range(rows):
        mix(r)
    for h in range(HEADS):
        attended_ref[:, pl.ds(h * HEAD_DIM, HEAD_DIM)] = mixed[pl.ds(h * rows, rows), :].astype(bf16)


def attend(plan, pieces, places, lengths, cosine, sine, key_cache, value_cache, fetched, width):
    rows, span, kv_width = key_cache.shape
    smem = pl.BlockSpec(memory_space=pltpu.SMEM)
    vmem = pl.BlockSpec(memory_space=pltpu.VMEM)
    return pl.pallas_call(
        functools.partial(attend_kernel, plan, rows, width // HEAD_DIM),
        out_shape=(
            jax.ShapeDtypeStruct((rows, HEADS * HEAD_DIM), bf16),
            jax.ShapeDtypeStruct((rows, 2 * KV_HEADS * HEAD_DIM), bf16),
        ),
        in_specs=[smem, smem] + [vmem] * (len(pieces) + 5),
        out_specs=(vmem, vmem),
        scratch_shapes=[
            pltpu.VMEM(((HEADS + 2 * KV_HEADS) * rows, HEAD_DIM), f32),
            pltpu.VMEM((rows, HEADS, span), f32),
            pltpu.VMEM((rows, HEADS, span), bf16),
            pltpu.VMEM((HEADS * rows, HEAD_DIM), f32),
        ],
        compiler_params=pltpu.CompilerParams(vmem_limit_bytes=12 * 2**20),
        name="attend",
    )(places, lengths, cosine, sine, *pieces, key_cache, value_cache, fetched)


def fetch_kernel(keys_hbm, values_hbm, keys, values, fetched, sems):
    loads = [
        pltpu.make_async_copy(keys_hbm, keys, sems.at[0]),
        pltpu.make_async_copy(values_hbm, values, sems.at[1]),
    ]
    for load in loads:
        load.start()
    for load in loads:
        load.wait()
    fetched[...] = jnp.zeros_like(fetched)


def fetch(key_cache, value_cache):
    vmem = pl.BlockSpec(memory_space=pltpu.VMEM)
    hbm = pl.BlockSpec(memory_space=pltpu.HBM)
    shape = jax.ShapeDtypeStruct(key_cache.shape, bf16)
    return pl.pallas_call(
        fetch_kernel,
        out_shape=(shape, shape, jax.ShapeDtypeStruct((8, 128), f32)),
        in_specs=[hbm, hbm],
        out_specs=(vmem, vmem, vmem),
        scratch_shapes=[pltpu.SemaphoreType.DMA((2,))],
        compiler_params=pltpu.CompilerParams(vmem_limit_bytes=16 * 2**20),
        name="fetch",
    )(key_cache, value_cache)


def rotation(lengths):
    half = HEAD_DIM // 2
    steps = jnp.arange(half, dtype=f32)
    inverse = jnp.exp(steps * (-2.0 * math.log(rope_base) / HEAD_DIM))
    angles = lengths.astype(f32)[:, None] * inverse[None, :]
    cosine = jnp.cos(angles)
    sine = jnp.sin(angles)
    return jnp.concatenate([cosine, cosine], axis=1), jnp.concatenate([-sine, sine], axis=1)


def body(hidden_states, norm_gain, projection_weight, key_cache, value_cache, lengths):
    along_x = lax.axis_size("gx")
    along_z = lax.axis_size("gy")
    chips = along_x // CORES
    rows = key_cache.shape[0]
    width = projection_weight.shape[1]
    z = lax.axis_index("gy").reshape(1).astype(jnp.int32)
    gx = lax.axis_index("gx")
    kept = along_z // 2
    first_rows = CORES * rows

    def on_gx(array, shift, flip):
        pairs = [
            ((x + shift) % chips * CORES + (c ^ flip), x * CORES + c)
            for x in range(chips)
            for c in range(CORES)
        ]
        return lax.ppermute(array, "gx", pairs)

    def on_z(array, flip):
        return lax.ppermute(array, "gy", [(s, s ^ flip) for s in range(along_z)])

    def in_hbm(array):
        return pltpu.with_memory_space_constraint(array, pltpu.HBM)

    gain = norm_gain.reshape(1, -1)
    weight = in_hbm(projection_weight)
    there = [on_gx(hidden_states, k, 0) for k in range(1, chips)]
    here = [(in_hbm(hidden_states), on_gx(hidden_states, 0, 1))]
    cosine, sine = rotation(lengths)

    unit = HEAD_DIM * 2
    if width % unit == 0 and width >= 4 * unit:
        own_cut, other_cut = split_at(width, unit, OWN_SHARE), split_at(width, unit, OTHER_SHARE)
    else:
        own_cut = other_cut = (width,)
    units = [(0, 0, own_cut[0], True)]
    for k in range(1, chips):
        units.append((k, 0, other_cut[0], True))
        units += [(k, other_cut[0], rest, False) for rest in other_cut[1:]]
    units += [(0, own_cut[0], rest, False) for rest in own_cut[1:]]

    def tie(*arrays):
        return lax.optimization_barrier(arrays)

    count = len(units)
    keeps, receiveds, owns, aways, arrived = [], [], [], [], []

    def add_pair(keep, received, squared):
        results = []
        for rest in (False, True):
            span = slice(first_rows, None) if rest else slice(0, first_rows)
            skip = HEAD_DIM if squared else 0
            parts = []
            if squared:
                square = (
                    keep[span, :HEAD_DIM]
                    + received[span, :HEAD_DIM].astype(f32)
                    + received[span, HEAD_DIM : 2 * HEAD_DIM].astype(f32)
                )
                upper = lax.reduce_precision(square, 8, 7)
                parts = [upper.astype(bf16), (square - upper).astype(bf16)] if rest else [square]
            total = keep[span, skip:] + received[span, 2 * skip :].astype(f32)
            results.append(parts + [total.astype(bf16) if rest else total])
        return results

    def step_one(u):
        own, away = add_pair(keeps[u], receiveds[u], units[u][3])
        owns.append(own)
        aways.append(jnp.concatenate(away, axis=1) if len(away) > 1 else away[0])

    def step_two(u):
        away = aways[u]
        arrived.append([on_z(away[(i - 1) * first_rows : i * first_rows], 2 * i) for i in range(1, kept)])

    sides = {0: here[0]}
    for u, (k, first, chunk, squared) in enumerate(units):
        if u > 1:
            receiveds[u - 2], keeps[u - 1] = tie(receiveds[u - 2], keeps[u - 1])
        if k not in sides:
            array, keeps[u - 1] = tie(there[k - 1], keeps[u - 1])
            sides[k] = (array, on_gx(array, 0, 1))
        a0, a1 = sides[k]
        if u:
            a0, keeps[u - 1] = tie(a0, keeps[u - 1])
        if u > 1:
            step_one(u - 2)
            a0, aways[u - 2] = tie(a0, aways[u - 2])
            step_two(u - 2)
        if u > 2:
            a0, arrived[u - 3] = tie(a0, arrived[u - 3])
        sides[k] = (a0, a1)
        keep, send = project(z, a0, a1, gain, weight, rows, first, chunk, squared)
        keeps.append(keep)
        receiveds.append(on_z(send, 1))
    plan, pieces, scales, projecteds = [], [], {}, []

    def finish(u):
        k, first, chunk, squared = units[u]
        own, others = owns[u], arrived[u]
        skip = 2 * HEAD_DIM if squared else 0
        if squared:
            square = own[0]
            for other in others:
                square = square + other[:, :HEAD_DIM].astype(f32) + other[:, HEAD_DIM:skip].astype(f32)
            scales[k] = lax.rsqrt(square[:, :1] * (1.0 / D) + norm_eps)
        total = own[-1]
        for other in others:
            total = total + other[:, skip:].astype(f32)
        projecteds.append((total * scales[k]).astype(bf16))

    def hand_out(u):
        k, first, chunk, _ = units[u]
        plan.append((k * CORES, first, chunk, 0))
        plan.append((k * CORES + 1, first, chunk, rows))
        held.append(on_gx(projecteds[u], chips - k, 0) if k else projecteds[u])

    held = []
    last = count - 1
    if count > 1:
        u = last - 1
        if u:
            receiveds[u], keeps[last], arrived[u - 1] = tie(receiveds[u], keeps[last], arrived[u - 1])
        step_one(u)
        *arrived[:], aways[u] = tie(*arrived, aways[u])
        step_two(u)
        for before in range(u):
            finish(before)
            hand_out(before)
        if u:
            receiveds[last], projecteds[-1], aways[u] = tie(receiveds[last], projecteds[-1], aways[u])
    step_one(last)
    if count > 1:
        arrived[last - 1], aways[last] = tie(arrived[last - 1], aways[last])
    step_two(last)
    if count > 1:
        finish(last - 1)
        hand_out(last - 1)
        projecteds[-1], key_cache = tie(projecteds[-1], key_cache)
    keys, values, fetched = fetch(in_hbm(key_cache), in_hbm(value_cache))
    *held[: last - 1], arrived[last], fetched = tie(*held[: last - 1], arrived[last], fetched)
    finish(last)
    hand_out(last)
    for projected in held:
        pieces.append(projected)
        pieces.append(on_gx(projected, 0, 1))
    x, core = gx // CORES, gx % CORES
    places = jnp.stack(
        [
            (x + chips - k) % chips * CORES + jnp.bitwise_xor(core, j)
            for k in range(chips)
            for j in range(CORES)
        ]
    ).astype(jnp.int32)
    return attend(
        plan, pieces, places, lengths, cosine, sine, keys, values, fetched, width
    )


def split_at(width, unit, share):
    first = round(width * share / unit) * unit
    return (first, width - first)


def solution(mesh):
    in_specs = (
        P(("groups", "gx"), "gy"),
        P("gy"),
        P("gy", "gx"),
        P(("groups", "gx", "gy"), None, None),
        P(("groups", "gx", "gy"), None, None),
        P(("groups", "gx", "gy")),
    )
    out_specs = (P(("groups", "gx", "gy"), None), P(("groups", "gx", "gy"), None))
    return jax.shard_map(body, mesh=mesh, in_specs=in_specs, out_specs=out_specs, check_vma=False)
```

```python
import functools
import math

import jax
import jax.numpy as jnp
from jax import lax
from jax.experimental import pallas as pl
from jax.experimental.pallas import tpu as pltpu
from jax.sharding import PartitionSpec as P

D = 16384
HEADS = 128
KV_HEADS = 8
HEAD_DIM = 128
GROUP = HEADS // KV_HEADS
CORES = 2
IN_FLIGHT = 3
OWN_SHARE = 0.56
OTHER_SHARE = 0.5

norm_eps = 1e-05
rope_base = 500000.0
f32 = jnp.float32
bf16 = jnp.bfloat16


def project_kernel(rows, kept, first, tiles, squared, z_ref, a0_ref, a1_ref, gain_ref, w_hbm, keep_hbm, send_ref, raw, acts, w, keep, row_sems, w_sems, keep_sems):
    half = kept * CORES * rows
    loads = []
    for m in range(2 * kept):
        source = pl.multiple_of(jnp.bitwise_xor(z_ref[0], m) * rows, rows)
        for j, ref in enumerate((a0_ref, a1_ref)):
            place = (m % 2) * half + ((m // 2) * CORES + j) * rows
            load = pltpu.make_async_copy(
                ref.at[pl.ds(source, rows), :], raw.at[pl.ds(place, rows), :], row_sems.at[m * CORES + j]
            )
            load.start()
            loads.append((place, load))
    copies = [
        pltpu.make_async_copy(
            w_hbm.at[:, pl.ds(first + begin, width)], w.at[:, pl.ds(begin, width)], w_sems.at[at]
        )
        for at, (begin, width) in enumerate(tiles)
    ]
    for copy in copies[:IN_FLIGHT]:
        copy.start()
    gain = gain_ref[...].astype(f32)
    offset = HEAD_DIM if squared else 0
    for place, load in loads:
        load.wait()
        block = raw[pl.ds(place, rows), :].astype(f32)
        acts[pl.ds(place, rows), :] = (block * gain).astype(bf16)
        if squared:
            square = jnp.broadcast_to(jnp.sum(block * block, axis=1, keepdims=True), (rows, HEAD_DIM))
            if place < half:
                keep[pl.ds(place, rows), pl.ds(0, HEAD_DIM)] = square
            else:
                upper = square.astype(bf16)
                send_ref[pl.ds(place - half, rows), pl.ds(0, HEAD_DIM)] = upper
                lower = (square - upper.astype(f32)).astype(bf16)
                send_ref[pl.ds(place - half, rows), pl.ds(HEAD_DIM, HEAD_DIM)] = lower
    stores = []
    for at, (copy, (begin, width)) in enumerate(zip(copies, tiles)):
        copy.wait()
        if at + IN_FLIGHT < len(copies):
            copies[at + IN_FLIGHT].start()
        total = jnp.dot(acts[...], w[:, pl.ds(begin, width)], preferred_element_type=f32)
        keep[:, pl.ds(offset + begin, width)] = total[:half]
        send_ref[:, pl.ds(2 * offset + begin, width)] = total[half:].astype(bf16)
        left = 0 if at == 0 else offset + begin
        columns = pl.ds(left, offset + begin + width - left)
        store = pltpu.make_async_copy(keep.at[:, columns], keep_hbm.at[:, columns], keep_sems.at[at])
        store.start()
        stores.append(store)
    for store in stores:
        store.wait()


def tiles_of(width):
    sizes = [256] if width % 256 == 0 else []
    while width > sum(sizes):
        sizes.append(min(512, width - sum(sizes)))
    return tuple((sum(sizes[:i]), size) for i, size in enumerate(sizes))


def project(z, a0, a1, gain, weight, rows, first, width, squared):
    depth = a0.shape[1]
    kept = a0.shape[0] // rows // 2
    half = kept * CORES * rows
    tiles = tiles_of(width)
    full = width + (HEAD_DIM if squared else 0)
    vmem = pl.BlockSpec(memory_space=pltpu.VMEM)
    hbm = pl.BlockSpec(memory_space=pltpu.HBM)
    return pl.pallas_call(
        functools.partial(project_kernel, rows, kept, first, tiles, squared),
        out_shape=(
            jax.ShapeDtypeStruct((half, full), f32),
            jax.ShapeDtypeStruct((half, 2 * full - width), bf16),
        ),
        in_specs=[pl.BlockSpec(memory_space=pltpu.SMEM), hbm, hbm, vmem, hbm],
        out_specs=(hbm, vmem),
        scratch_shapes=[
            pltpu.VMEM((2 * half, depth), bf16),
            pltpu.VMEM((2 * half, depth), bf16),
            pltpu.VMEM((depth, width), bf16),
            pltpu.VMEM((half, full), f32),
            pltpu.SemaphoreType.DMA((2 * kept * CORES,)),
            pltpu.SemaphoreType.DMA((len(tiles),)),
            pltpu.SemaphoreType.DMA((len(tiles),)),
        ],
        compiler_params=pltpu.CompilerParams(vmem_limit_bytes=32 * 2**20),
        name="project",
    )(z, a0, a1, gain, weight)


def attend_kernel(plan, rows, per_source, *refs):
    count = len(plan)
    places_ref, lengths_ref, cosine_ref, sine_ref = refs[:4]
    pieces = refs[4 : 4 + count]
    keys, values, _, attended_ref, cache_rows_ref = refs[4 + count : 9 + count]
    heads, scores_ref, weights_ref, mixed = refs[9 + count :]
    cosine = cosine_ref[...]
    sine = sine_ref[...]
    rotated = HEADS + KV_HEADS
    for (source, first, width, start), piece in zip(plan, pieces):
        for column in range(0, width, HEAD_DIM):
            local = (first + column) // HEAD_DIM
            h = places_ref[source] * per_source + local
            head = piece[pl.ds(start, rows), pl.ds(column, HEAD_DIM)].astype(f32)
            turned = head * cosine + pltpu.roll(head, HEAD_DIM // 2, 1) * sine
            if local + KV_HEADS >= per_source:
                turned = jnp.where(h < rotated, turned, head)
            heads[pl.ds(pl.multiple_of(h * rows, rows), rows), :] = turned.astype(bf16).astype(f32)
    for h in range(2 * KV_HEADS):
        cache_rows_ref[:, pl.ds(h * HEAD_DIM, HEAD_DIM)] = heads[pl.ds((HEADS + h) * rows, rows), :].astype(bf16)
    span = keys.shape[1]
    position = lax.broadcasted_iota(jnp.int32, (HEADS, span), 1)

    def score(r):
        query = heads[pl.ds(r, HEADS, stride=rows), :].astype(bf16)
        empty = jnp.zeros((GROUP, HEAD_DIM), bf16)
        for k in range(0, KV_HEADS, 2):
            front = jnp.concatenate([query[k * GROUP : (k + 1) * GROUP], empty], axis=1)
            second = jnp.concatenate([empty, query[(k + 1) * GROUP : (k + 2) * GROUP]], axis=1)
            scores_ref[r, pl.ds(k * GROUP, 2 * GROUP), :] = lax.dot_general(
                jnp.concatenate([front, second], axis=0),
                keys[r, :, pl.ds(k * HEAD_DIM, 2 * HEAD_DIM)],
                (((1,), (1,)), ((), ())),
                preferred_element_type=f32,
            )

    def soften(r):
        query = heads[pl.ds(r, HEADS, stride=rows), :]
        own_key = heads[pl.ds(HEADS * rows + r, KV_HEADS, stride=rows), :]
        own_value = heads[pl.ds((HEADS + KV_HEADS) * rows + r, KV_HEADS, stride=rows), :]
        spread = jnp.concatenate(
            [jnp.broadcast_to(own_key[k : k + 1], (GROUP, HEAD_DIM)) for k in range(KV_HEADS)], axis=0
        )
        own_score = jnp.sum(query * spread, axis=1, keepdims=True) * HEAD_DIM ** (-0.5)
        masked = jnp.where(position < lengths_ref[r], scores_ref[r] * HEAD_DIM ** (-0.5), -jnp.inf)
        top = jnp.maximum(jnp.max(masked, axis=1, keepdims=True), own_score)
        raised = jnp.exp(masked - top)
        raised_own = jnp.exp(own_score - top)
        inverse = 1.0 / (jnp.sum(raised, axis=1, keepdims=True) + raised_own)
        weights_ref[r] = (raised * inverse).astype(bf16)
        own_weight = (raised_own * inverse).astype(bf16).astype(f32)
        spread = jnp.concatenate(
            [jnp.broadcast_to(own_value[k : k + 1], (GROUP, HEAD_DIM)) for k in range(KV_HEADS)], axis=0
        )
        scores_ref[r] = own_weight * spread

    def mix(r):
        for k in range(0, KV_HEADS, 2):
            both = jnp.dot(
                weights_ref[r, pl.ds(k * GROUP, 2 * GROUP), :],
                values[r, :, pl.ds(k * HEAD_DIM, 2 * HEAD_DIM)],
                preferred_element_type=f32,
            )
            for i in range(2):
                mixed[pl.ds((k + i) * GROUP * rows + r, GROUP, stride=rows), :] = (
                    both[i * GROUP : (i + 1) * GROUP, i * HEAD_DIM : (i + 1) * HEAD_DIM]
                    + scores_ref[r, pl.ds((k + i) * GROUP, GROUP), :]
                )

    for r in range(rows):
        score(r)
    for r in range(rows):
        soften(r)
    for r in range(rows):
        mix(r)
    for h in range(HEADS):
        attended_ref[:, pl.ds(h * HEAD_DIM, HEAD_DIM)] = mixed[pl.ds(h * rows, rows), :].astype(bf16)


def attend(plan, pieces, places, lengths, cosine, sine, key_cache, value_cache, fetched, width):
    rows, span, kv_width = key_cache.shape
    smem = pl.BlockSpec(memory_space=pltpu.SMEM)
    vmem = pl.BlockSpec(memory_space=pltpu.VMEM)
    return pl.pallas_call(
        functools.partial(attend_kernel, plan, rows, width // HEAD_DIM),
        out_shape=(
            jax.ShapeDtypeStruct((rows, HEADS * HEAD_DIM), bf16),
            jax.ShapeDtypeStruct((rows, 2 * KV_HEADS * HEAD_DIM), bf16),
        ),
        in_specs=[smem, smem] + [vmem] * (len(pieces) + 5),
        out_specs=(vmem, vmem),
        scratch_shapes=[
            pltpu.VMEM(((HEADS + 2 * KV_HEADS) * rows, HEAD_DIM), f32),
            pltpu.VMEM((rows, HEADS, span), f32),
            pltpu.VMEM((rows, HEADS, span), bf16),
            pltpu.VMEM((HEADS * rows, HEAD_DIM), f32),
        ],
        compiler_params=pltpu.CompilerParams(vmem_limit_bytes=12 * 2**20),
        name="attend",
    )(places, lengths, cosine, sine, *pieces, key_cache, value_cache, fetched)


def fetch_kernel(keys_hbm, values_hbm, keys, values, fetched, sems):
    loads = [
        pltpu.make_async_copy(keys_hbm, keys, sems.at[0]),
        pltpu.make_async_copy(values_hbm, values, sems.at[1]),
    ]
    for load in loads:
        load.start()
    for load in loads:
        load.wait()
    fetched[...] = jnp.zeros_like(fetched)


def fetch(key_cache, value_cache):
    vmem = pl.BlockSpec(memory_space=pltpu.VMEM)
    hbm = pl.BlockSpec(memory_space=pltpu.HBM)
    shape = jax.ShapeDtypeStruct(key_cache.shape, bf16)
    return pl.pallas_call(
        fetch_kernel,
        out_shape=(shape, shape, jax.ShapeDtypeStruct((8, 128), f32)),
        in_specs=[hbm, hbm],
        out_specs=(vmem, vmem, vmem),
        scratch_shapes=[pltpu.SemaphoreType.DMA((2,))],
        compiler_params=pltpu.CompilerParams(vmem_limit_bytes=16 * 2**20),
        name="fetch",
    )(key_cache, value_cache)


def rotation(lengths):
    half = HEAD_DIM // 2
    steps = jnp.arange(half, dtype=f32)
    inverse = jnp.exp(steps * (-2.0 * math.log(rope_base) / HEAD_DIM))
    angles = lengths.astype(f32)[:, None] * inverse[None, :]
    cosine = jnp.cos(angles)
    sine = jnp.sin(angles)
    return jnp.concatenate([cosine, cosine], axis=1), jnp.concatenate([-sine, sine], axis=1)


def body(hidden_states, norm_gain, projection_weight, key_cache, value_cache, lengths):
    along_x = lax.axis_size("gx")
    along_z = lax.axis_size("gy")
    chips = along_x // CORES
    rows = key_cache.shape[0]
    width = projection_weight.shape[1]
    z = lax.axis_index("gy").reshape(1).astype(jnp.int32)
    gx = lax.axis_index("gx")
    kept = along_z // 2
    first_rows = CORES * rows

    def on_gx(array, shift, flip):
        pairs = [
            ((x + shift) % chips * CORES + (c ^ flip), x * CORES + c)
            for x in range(chips)
            for c in range(CORES)
        ]
        return lax.ppermute(array, "gx", pairs)

    def on_z(array, flip):
        return lax.ppermute(array, "gy", [(s, s ^ flip) for s in range(along_z)])

    def in_hbm(array):
        return pltpu.with_memory_space_constraint(array, pltpu.HBM)

    gain = norm_gain.reshape(1, -1)
    weight = in_hbm(projection_weight)
    there = [on_gx(hidden_states, k, 0) for k in range(1, chips)]
    here = [(in_hbm(hidden_states), on_gx(hidden_states, 0, 1))]
    cosine, sine = rotation(lengths)

    unit = HEAD_DIM * 2
    if width % unit == 0 and width >= 4 * unit:
        own_cut, other_cut = split_at(width, unit, OWN_SHARE), split_at(width, unit, OTHER_SHARE)
    else:
        own_cut = other_cut = (width,)
    units = [(0, 0, own_cut[0], True)]
    for k in range(1, chips):
        units.append((k, 0, other_cut[0], True))
        units += [(k, other_cut[0], rest, False) for rest in other_cut[1:]]
    units += [(0, own_cut[0], rest, False) for rest in own_cut[1:]]

    def tie(*arrays):
        return lax.optimization_barrier(arrays)

    count = len(units)
    keeps, receiveds, owns, aways, arrived = [], [], [], [], []

    def add_pair(keep, received, squared):
        results = []
        for rest in (False, True):
            span = slice(first_rows, None) if rest else slice(0, first_rows)
            skip = HEAD_DIM if squared else 0
            parts = []
            if squared:
                square = (
                    keep[span, :HEAD_DIM]
                    + received[span, :HEAD_DIM].astype(f32)
                    + received[span, HEAD_DIM : 2 * HEAD_DIM].astype(f32)
                )
                upper = lax.reduce_precision(square, 8, 7)
                parts = [upper.astype(bf16), (square - upper).astype(bf16)] if rest else [square]
            total = keep[span, skip:] + received[span, 2 * skip :].astype(f32)
            results.append(parts + [total.astype(bf16) if rest else total])
        return results

    def step_one(u):
        own, away = add_pair(keeps[u], receiveds[u], units[u][3])
        owns.append(own)
        aways.append(jnp.concatenate(away, axis=1) if len(away) > 1 else away[0])

    def step_two(u):
        away = aways[u]
        arrived.append([on_z(away[(i - 1) * first_rows : i * first_rows], 2 * i) for i in range(1, kept)])

    sides = {0: here[0]}
    for u, (k, first, chunk, squared) in enumerate(units):
        if u > 1:
            receiveds[u - 2], keeps[u - 1] = tie(receiveds[u - 2], keeps[u - 1])
        if k not in sides:
            array, keeps[u - 1] = tie(there[k - 1], keeps[u - 1])
            sides[k] = (array, on_gx(array, 0, 1))
        a0, a1 = sides[k]
        if u:
            a0, keeps[u - 1] = tie(a0, keeps[u - 1])
        if u > 1:
            step_one(u - 2)
            a0, aways[u - 2] = tie(a0, aways[u - 2])
            step_two(u - 2)
        if u > 2:
            a0, arrived[u - 3] = tie(a0, arrived[u - 3])
        sides[k] = (a0, a1)
        keep, send = project(z, a0, a1, gain, weight, rows, first, chunk, squared)
        keeps.append(keep)
        receiveds.append(on_z(send, 1))
    plan, pieces, scales, projecteds = [], [], {}, []

    def finish(u):
        k, first, chunk, squared = units[u]
        own, others = owns[u], arrived[u]
        skip = 2 * HEAD_DIM if squared else 0
        if squared:
            square = own[0]
            for other in others:
                square = square + other[:, :HEAD_DIM].astype(f32) + other[:, HEAD_DIM:skip].astype(f32)
            scales[k] = lax.rsqrt(square[:, :1] * (1.0 / D) + norm_eps)
        total = own[-1]
        for other in others:
            total = total + other[:, skip:].astype(f32)
        projecteds.append((total * scales[k]).astype(bf16))

    def hand_out(u):
        k, first, chunk, _ = units[u]
        plan.append((k * CORES, first, chunk, 0))
        plan.append((k * CORES + 1, first, chunk, rows))
        held.append(on_gx(projecteds[u], chips - k, 0) if k else projecteds[u])

    held = []
    last = count - 1
    if count > 1:
        u = last - 1
        if u:
            receiveds[u], keeps[last], arrived[u - 1] = tie(receiveds[u], keeps[last], arrived[u - 1])
        step_one(u)
        *arrived[:], aways[u] = tie(*arrived, aways[u])
        step_two(u)
        for before in range(u):
            finish(before)
            hand_out(before)
        if u:
            receiveds[last], projecteds[-1], aways[u] = tie(receiveds[last], projecteds[-1], aways[u])
    step_one(last)
    if count > 1:
        arrived[last - 1], aways[last] = tie(arrived[last - 1], aways[last])
    step_two(last)
    if count > 1:
        finish(last - 1)
        hand_out(last - 1)
        projecteds[-1], key_cache = tie(projecteds[-1], key_cache)
    keys, values, fetched = fetch(in_hbm(key_cache), in_hbm(value_cache))
    *held[: last - 1], arrived[last], fetched = tie(*held[: last - 1], arrived[last], fetched)
    finish(last)
    hand_out(last)
    for projected in held:
        pieces.append(projected)
        pieces.append(on_gx(projected, 0, 1))
    x, core = gx // CORES, gx % CORES
    places = jnp.stack(
        [
            (x + chips - k) % chips * CORES + jnp.bitwise_xor(core, j)
            for k in range(chips)
            for j in range(CORES)
        ]
    ).astype(jnp.int32)
    return attend(
        plan, pieces, places, lengths, cosine, sine, keys, values, fetched, width
    )


def split_at(width, unit, share):
    first = round(width * share / unit) * unit
    return (first, width - first)


def solution(mesh):
    in_specs = (
        P(("groups", "gx"), "gy"),
        P("gy"),
        P("gy", "gx"),
        P(("groups", "gx", "gy"), None, None),
        P(("groups", "gx", "gy"), None, None),
        P(("groups", "gx", "gy")),
    )
    out_specs = (P(("groups", "gx", "gy"), None), P(("groups", "gx", "gy"), None))
    return jax.shard_map(body, mesh=mesh, in_specs=in_specs, out_specs=out_specs, check_vma=False)
```

```python
import functools
import math

import jax
import jax.numpy as jnp
from jax import lax
from jax.experimental import pallas as pl
from jax.experimental.pallas import tpu as pltpu
from jax.sharding import PartitionSpec as P

D = 16384
HEADS = 128
KV_HEADS = 8
HEAD_DIM = 128
GROUP = HEADS // KV_HEADS
CORES = 2
IN_FLIGHT = 3
OWN_SHARE = 0.56
OTHER_SHARE = 0.5

norm_eps = 1e-05
rope_base = 500000.0
f32 = jnp.float32
bf16 = jnp.bfloat16


def project_kernel(rows, kept, first, tiles, squared, z_ref, a0_ref, a1_ref, gain_ref, w_hbm, keep_hbm, send_ref, raw, acts, w, keep, row_sems, w_sems, keep_sems):
    half = kept * CORES * rows
    loads = []
    for m in range(2 * kept):
        source = pl.multiple_of(jnp.bitwise_xor(z_ref[0], m) * rows, rows)
        for j, ref in enumerate((a0_ref, a1_ref)):
            place = (m % 2) * half + ((m // 2) * CORES + j) * rows
            load = pltpu.make_async_copy(
                ref.at[pl.ds(source, rows), :], raw.at[pl.ds(place, rows), :], row_sems.at[m * CORES + j]
            )
            load.start()
            loads.append((place, load))
    copies = [
        pltpu.make_async_copy(
            w_hbm.at[:, pl.ds(first + begin, width)], w.at[:, pl.ds(begin, width)], w_sems.at[at]
        )
        for at, (begin, width) in enumerate(tiles)
    ]
    for copy in copies[:IN_FLIGHT]:
        copy.start()
    gain = gain_ref[...].astype(f32)
    offset = HEAD_DIM if squared else 0
    for place, load in loads:
        load.wait()
        block = raw[pl.ds(place, rows), :].astype(f32)
        acts[pl.ds(place, rows), :] = (block * gain).astype(bf16)
        if squared:
            square = jnp.broadcast_to(jnp.sum(block * block, axis=1, keepdims=True), (rows, HEAD_DIM))
            if place < half:
                keep[pl.ds(place, rows), pl.ds(0, HEAD_DIM)] = square
            else:
                upper = square.astype(bf16)
                send_ref[pl.ds(place - half, rows), pl.ds(0, HEAD_DIM)] = upper
                lower = (square - upper.astype(f32)).astype(bf16)
                send_ref[pl.ds(place - half, rows), pl.ds(HEAD_DIM, HEAD_DIM)] = lower
    stores = []
    for at, (copy, (begin, width)) in enumerate(zip(copies, tiles)):
        copy.wait()
        if at + IN_FLIGHT < len(copies):
            copies[at + IN_FLIGHT].start()
        total = jnp.dot(acts[...], w[:, pl.ds(begin, width)], preferred_element_type=f32)
        keep[:, pl.ds(offset + begin, width)] = total[:half]
        send_ref[:, pl.ds(2 * offset + begin, width)] = total[half:].astype(bf16)
        left = 0 if at == 0 else offset + begin
        columns = pl.ds(left, offset + begin + width - left)
        store = pltpu.make_async_copy(keep.at[:, columns], keep_hbm.at[:, columns], keep_sems.at[at])
        store.start()
        stores.append(store)
    for store in stores:
        store.wait()


def tiles_of(width):
    sizes = [256] if width % 256 == 0 else []
    while width > sum(sizes):
        sizes.append(min(512, width - sum(sizes)))
    return tuple((sum(sizes[:i]), size) for i, size in enumerate(sizes))


def project(z, a0, a1, gain, weight, rows, first, width, squared):
    depth = a0.shape[1]
    kept = a0.shape[0] // rows // 2
    half = kept * CORES * rows
    tiles = tiles_of(width)
    full = width + (HEAD_DIM if squared else 0)
    vmem = pl.BlockSpec(memory_space=pltpu.VMEM)
    hbm = pl.BlockSpec(memory_space=pltpu.HBM)
    return pl.pallas_call(
        functools.partial(project_kernel, rows, kept, first, tiles, squared),
        out_shape=(
            jax.ShapeDtypeStruct((half, full), f32),
            jax.ShapeDtypeStruct((half, 2 * full - width), bf16),
        ),
        in_specs=[pl.BlockSpec(memory_space=pltpu.SMEM), hbm, hbm, vmem, hbm],
        out_specs=(hbm, vmem),
        scratch_shapes=[
            pltpu.VMEM((2 * half, depth), bf16),
            pltpu.VMEM((2 * half, depth), bf16),
            pltpu.VMEM((depth, width), bf16),
            pltpu.VMEM((half, full), f32),
            pltpu.SemaphoreType.DMA((2 * kept * CORES,)),
            pltpu.SemaphoreType.DMA((len(tiles),)),
            pltpu.SemaphoreType.DMA((len(tiles),)),
        ],
        compiler_params=pltpu.CompilerParams(vmem_limit_bytes=32 * 2**20),
        name="project",
    )(z, a0, a1, gain, weight)


def attend_kernel(plan, rows, per_source, *refs):
    count = len(plan)
    places_ref, lengths_ref, cosine_ref, sine_ref = refs[:4]
    pieces = refs[4 : 4 + count]
    keys, values, _, attended_ref, cache_rows_ref = refs[4 + count : 9 + count]
    heads, scores_ref, weights_ref, mixed = refs[9 + count :]
    cosine = cosine_ref[...]
    sine = sine_ref[...]
    rotated = HEADS + KV_HEADS
    for (source, first, width, start), piece in zip(plan, pieces):
        for column in range(0, width, HEAD_DIM):
            local = (first + column) // HEAD_DIM
            h = places_ref[source] * per_source + local
            head = piece[pl.ds(start, rows), pl.ds(column, HEAD_DIM)].astype(f32)
            turned = head * cosine + pltpu.roll(head, HEAD_DIM // 2, 1) * sine
            if local + KV_HEADS >= per_source:
                turned = jnp.where(h < rotated, turned, head)
            heads[pl.ds(pl.multiple_of(h * rows, rows), rows), :] = turned.astype(bf16).astype(f32)
    for h in range(2 * KV_HEADS):
        cache_rows_ref[:, pl.ds(h * HEAD_DIM, HEAD_DIM)] = heads[pl.ds((HEADS + h) * rows, rows), :].astype(bf16)
    span = keys.shape[1]
    position = lax.broadcasted_iota(jnp.int32, (HEADS, span), 1)

    def score(r):
        query = heads[pl.ds(r, HEADS, stride=rows), :].astype(bf16)
        empty = jnp.zeros((GROUP, HEAD_DIM), bf16)
        for k in range(0, KV_HEADS, 2):
            front = jnp.concatenate([query[k * GROUP : (k + 1) * GROUP], empty], axis=1)
            second = jnp.concatenate([empty, query[(k + 1) * GROUP : (k + 2) * GROUP]], axis=1)
            scores_ref[r, pl.ds(k * GROUP, 2 * GROUP), :] = lax.dot_general(
                jnp.concatenate([front, second], axis=0),
                keys[r, :, pl.ds(k * HEAD_DIM, 2 * HEAD_DIM)],
                (((1,), (1,)), ((), ())),
                preferred_element_type=f32,
            )

    def soften(r):
        query = heads[pl.ds(r, HEADS, stride=rows), :]
        own_key = heads[pl.ds(HEADS * rows + r, KV_HEADS, stride=rows), :]
        own_value = heads[pl.ds((HEADS + KV_HEADS) * rows + r, KV_HEADS, stride=rows), :]
        spread = jnp.concatenate(
            [jnp.broadcast_to(own_key[k : k + 1], (GROUP, HEAD_DIM)) for k in range(KV_HEADS)], axis=0
        )
        own_score = jnp.sum(query * spread, axis=1, keepdims=True) * HEAD_DIM ** (-0.5)
        masked = jnp.where(position < lengths_ref[r], scores_ref[r] * HEAD_DIM ** (-0.5), -jnp.inf)
        top = jnp.maximum(jnp.max(masked, axis=1, keepdims=True), own_score)
        raised = jnp.exp(masked - top)
        raised_own = jnp.exp(own_score - top)
        inverse = 1.0 / (jnp.sum(raised, axis=1, keepdims=True) + raised_own)
        weights_ref[r] = (raised * inverse).astype(bf16)
        own_weight = (raised_own * inverse).astype(bf16).astype(f32)
        spread = jnp.concatenate(
            [jnp.broadcast_to(own_value[k : k + 1], (GROUP, HEAD_DIM)) for k in range(KV_HEADS)], axis=0
        )
        scores_ref[r] = own_weight * spread

    def mix(r):
        for k in range(0, KV_HEADS, 2):
            both = jnp.dot(
                weights_ref[r, pl.ds(k * GROUP, 2 * GROUP), :],
                values[r, :, pl.ds(k * HEAD_DIM, 2 * HEAD_DIM)],
                preferred_element_type=f32,
            )
            for i in range(2):
                mixed[pl.ds((k + i) * GROUP * rows + r, GROUP, stride=rows), :] = (
                    both[i * GROUP : (i + 1) * GROUP, i * HEAD_DIM : (i + 1) * HEAD_DIM]
                    + scores_ref[r, pl.ds((k + i) * GROUP, GROUP), :]
                )

    for r in range(rows):
        score(r)
    for r in range(rows):
        soften(r)
    for r in range(rows):
        mix(r)
    for h in range(HEADS):
        attended_ref[:, pl.ds(h * HEAD_DIM, HEAD_DIM)] = mixed[pl.ds(h * rows, rows), :].astype(bf16)


def attend(plan, pieces, places, lengths, cosine, sine, key_cache, value_cache, fetched, width):
    rows, span, kv_width = key_cache.shape
    smem = pl.BlockSpec(memory_space=pltpu.SMEM)
    vmem = pl.BlockSpec(memory_space=pltpu.VMEM)
    return pl.pallas_call(
        functools.partial(attend_kernel, plan, rows, width // HEAD_DIM),
        out_shape=(
            jax.ShapeDtypeStruct((rows, HEADS * HEAD_DIM), bf16),
            jax.ShapeDtypeStruct((rows, 2 * KV_HEADS * HEAD_DIM), bf16),
        ),
        in_specs=[smem, smem] + [vmem] * (len(pieces) + 5),
        out_specs=(vmem, vmem),
        scratch_shapes=[
            pltpu.VMEM(((HEADS + 2 * KV_HEADS) * rows, HEAD_DIM), f32),
            pltpu.VMEM((rows, HEADS, span), f32),
            pltpu.VMEM((rows, HEADS, span), bf16),
            pltpu.VMEM((HEADS * rows, HEAD_DIM), f32),
        ],
        compiler_params=pltpu.CompilerParams(vmem_limit_bytes=12 * 2**20),
        name="attend",
    )(places, lengths, cosine, sine, *pieces, key_cache, value_cache, fetched)


def fetch_kernel(keys_hbm, values_hbm, keys, values, fetched, sems):
    loads = [
        pltpu.make_async_copy(keys_hbm, keys, sems.at[0]),
        pltpu.make_async_copy(values_hbm, values, sems.at[1]),
    ]
    for load in loads:
        load.start()
    for load in loads:
        load.wait()
    fetched[...] = jnp.zeros_like(fetched)


def fetch(key_cache, value_cache):
    vmem = pl.BlockSpec(memory_space=pltpu.VMEM)
    hbm = pl.BlockSpec(memory_space=pltpu.HBM)
    shape = jax.ShapeDtypeStruct(key_cache.shape, bf16)
    return pl.pallas_call(
        fetch_kernel,
        out_shape=(shape, shape, jax.ShapeDtypeStruct((8, 128), f32)),
        in_specs=[hbm, hbm],
        out_specs=(vmem, vmem, vmem),
        scratch_shapes=[pltpu.SemaphoreType.DMA((2,))],
        compiler_params=pltpu.CompilerParams(vmem_limit_bytes=16 * 2**20),
        name="fetch",
    )(key_cache, value_cache)


def rotation(lengths):
    half = HEAD_DIM // 2
    steps = jnp.arange(half, dtype=f32)
    inverse = jnp.exp(steps * (-2.0 * math.log(rope_base) / HEAD_DIM))
    angles = lengths.astype(f32)[:, None] * inverse[None, :]
    cosine = jnp.cos(angles)
    sine = jnp.sin(angles)
    return jnp.concatenate([cosine, cosine], axis=1), jnp.concatenate([-sine, sine], axis=1)


def body(hidden_states, norm_gain, projection_weight, key_cache, value_cache, lengths):
    along_x = lax.axis_size("gx")
    along_z = lax.axis_size("gy")
    chips = along_x // CORES
    rows = key_cache.shape[0]
    width = projection_weight.shape[1]
    z = lax.axis_index("gy").reshape(1).astype(jnp.int32)
    gx = lax.axis_index("gx")
    kept = along_z // 2
    first_rows = CORES * rows

    def on_gx(array, shift, flip):
        pairs = [
            ((x + shift) % chips * CORES + (c ^ flip), x * CORES + c)
            for x in range(chips)
            for c in range(CORES)
        ]
        return lax.ppermute(array, "gx", pairs)

    def on_z(array, flip):
        return lax.ppermute(array, "gy", [(s, s ^ flip) for s in range(along_z)])

    def in_hbm(array):
        return pltpu.with_memory_space_constraint(array, pltpu.HBM)

    gain = norm_gain.reshape(1, -1)
    weight = in_hbm(projection_weight)
    there = [on_gx(hidden_states, k, 0) for k in range(1, chips)]
    here = [(in_hbm(hidden_states), on_gx(hidden_states, 0, 1))]
    cosine, sine = rotation(lengths)

    unit = HEAD_DIM * 2
    if width % unit == 0 and width >= 4 * unit:
        own_cut, other_cut = split_at(width, unit, OWN_SHARE), split_at(width, unit, OTHER_SHARE)
    else:
        own_cut = other_cut = (width,)
    units = [(0, 0, own_cut[0], True)]
    for k in range(1, chips):
        units.append((k, 0, other_cut[0], True))
        units += [(k, other_cut[0], rest, False) for rest in other_cut[1:]]
    units += [(0, own_cut[0], rest, False) for rest in own_cut[1:]]

    def tie(*arrays):
        return lax.optimization_barrier(arrays)

    count = len(units)
    keeps, receiveds, owns, aways, arrived = [], [], [], [], []

    def add_pair(keep, received, squared):
        results = []
        for rest in (False, True):
            span = slice(first_rows, None) if rest else slice(0, first_rows)
            skip = HEAD_DIM if squared else 0
            parts = []
            if squared:
                square = (
                    keep[span, :HEAD_DIM]
                    + received[span, :HEAD_DIM].astype(f32)
                    + received[span, HEAD_DIM : 2 * HEAD_DIM].astype(f32)
                )
                upper = lax.reduce_precision(square, 8, 7)
                parts = [upper.astype(bf16), (square - upper).astype(bf16)] if rest else [square]
            total = keep[span, skip:] + received[span, 2 * skip :].astype(f32)
            results.append(parts + [total.astype(bf16) if rest else total])
        return results

    def step_one(u):
        own, away = add_pair(keeps[u], receiveds[u], units[u][3])
        owns.append(own)
        aways.append(jnp.concatenate(away, axis=1) if len(away) > 1 else away[0])

    def step_two(u):
        away = aways[u]
        arrived.append([on_z(away[(i - 1) * first_rows : i * first_rows], 2 * i) for i in range(1, kept)])

    sides = {0: here[0]}
    for u, (k, first, chunk, squared) in enumerate(units):
        if u > 1:
            receiveds[u - 2], keeps[u - 1] = tie(receiveds[u - 2], keeps[u - 1])
        if k not in sides:
            array, keeps[u - 1] = tie(there[k - 1], keeps[u - 1])
            sides[k] = (array, on_gx(array, 0, 1))
        a0, a1 = sides[k]
        if u:
            a0, keeps[u - 1] = tie(a0, keeps[u - 1])
        if u > 1:
            step_one(u - 2)
            a0, aways[u - 2] = tie(a0, aways[u - 2])
            step_two(u - 2)
        if u > 2:
            a0, arrived[u - 3] = tie(a0, arrived[u - 3])
        sides[k] = (a0, a1)
        keep, send = project(z, a0, a1, gain, weight, rows, first, chunk, squared)
        keeps.append(keep)
        receiveds.append(on_z(send, 1))
    plan, pieces, scales, projecteds = [], [], {}, []

    def finish(u):
        k, first, chunk, squared = units[u]
        own, others = owns[u], arrived[u]
        skip = 2 * HEAD_DIM if squared else 0
        if squared:
            square = own[0]
            for other in others:
                square = square + other[:, :HEAD_DIM].astype(f32) + other[:, HEAD_DIM:skip].astype(f32)
            scales[k] = lax.rsqrt(square[:, :1] * (1.0 / D) + norm_eps)
        total = own[-1]
        for other in others:
            total = total + other[:, skip:].astype(f32)
        projecteds.append((total * scales[k]).astype(bf16))

    def hand_out(u):
        k, first, chunk, _ = units[u]
        plan.append((k * CORES, first, chunk, 0))
        plan.append((k * CORES + 1, first, chunk, rows))
        held.append(on_gx(projecteds[u], chips - k, 0) if k else projecteds[u])

    held = []
    last = count - 1
    if count > 1:
        u = last - 1
        if u:
            receiveds[u], keeps[last], arrived[u - 1] = tie(receiveds[u], keeps[last], arrived[u - 1])
        step_one(u)
        *arrived[:], aways[u] = tie(*arrived, aways[u])
        step_two(u)
        for before in range(u):
            finish(before)
            hand_out(before)
        aways[u], key_cache = tie(aways[u], key_cache)
        keys, values, fetched = fetch(in_hbm(key_cache), in_hbm(value_cache))
        if u:
            receiveds[last], projecteds[-1], aways[u], fetched = tie(receiveds[last], projecteds[-1], aways[u], fetched)
    step_one(last)
    if count > 1:
        arrived[last - 1], aways[last] = tie(arrived[last - 1], aways[last])
    step_two(last)
    if count > 1:
        finish(last - 1)
        hand_out(last - 1)
    else:
        keys, values, fetched = fetch(in_hbm(key_cache), in_hbm(value_cache))
    *held[: last - 1], arrived[last], fetched = tie(*held[: last - 1], arrived[last], fetched)
    finish(last)
    hand_out(last)
    for projected in held:
        pieces.append(projected)
        pieces.append(on_gx(projected, 0, 1))
    x, core = gx // CORES, gx % CORES
    places = jnp.stack(
        [
            (x + chips - k) % chips * CORES + jnp.bitwise_xor(core, j)
            for k in range(chips)
            for j in range(CORES)
        ]
    ).astype(jnp.int32)
    return attend(
        plan, pieces, places, lengths, cosine, sine, keys, values, fetched, width
    )


def split_at(width, unit, share):
    first = round(width * share / unit) * unit
    return (first, width - first)


def solution(mesh):
    in_specs = (
        P(("groups", "gx"), "gy"),
        P("gy"),
        P("gy", "gx"),
        P(("groups", "gx", "gy"), None, None),
        P(("groups", "gx", "gy"), None, None),
        P(("groups", "gx", "gy")),
    )
    out_specs = (P(("groups", "gx", "gy"), None), P(("groups", "gx", "gy"), None))
    return jax.shard_map(body, mesh=mesh, in_specs=in_specs, out_specs=out_specs, check_vma=False)
```

```python
import functools
import math

import jax
import jax.numpy as jnp
from jax import lax
from jax.experimental import pallas as pl
from jax.experimental.pallas import tpu as pltpu
from jax.sharding import PartitionSpec as P

D = 16384
HEADS = 128
KV_HEADS = 8
HEAD_DIM = 128
GROUP = HEADS // KV_HEADS
CORES = 2
IN_FLIGHT = 4
OWN_SHARE = 0.56
OTHER_SHARE = 0.5

norm_eps = 1e-05
rope_base = 500000.0
f32 = jnp.float32
bf16 = jnp.bfloat16


def project_kernel(rows, kept, first, tiles, squared, z_ref, a0_ref, a1_ref, gain_ref, w_hbm, keep_hbm, send_ref, raw, acts, w, keep, row_sems, w_sems, keep_sems):
    half = kept * CORES * rows
    loads = []
    for m in range(2 * kept):
        source = pl.multiple_of(jnp.bitwise_xor(z_ref[0], m) * rows, rows)
        for j, ref in enumerate((a0_ref, a1_ref)):
            place = (m % 2) * half + ((m // 2) * CORES + j) * rows
            load = pltpu.make_async_copy(
                ref.at[pl.ds(source, rows), :], raw.at[pl.ds(place, rows), :], row_sems.at[m * CORES + j]
            )
            load.start()
            loads.append((place, load))
    copies = [
        pltpu.make_async_copy(
            w_hbm.at[:, pl.ds(first + begin, width)], w.at[:, pl.ds(begin, width)], w_sems.at[at]
        )
        for at, (begin, width) in enumerate(tiles)
    ]
    for copy in copies[:IN_FLIGHT]:
        copy.start()
    gain = gain_ref[...].astype(f32)
    offset = HEAD_DIM if squared else 0
    for place, load in loads:
        load.wait()
        block = raw[pl.ds(place, rows), :].astype(f32)
        acts[pl.ds(place, rows), :] = (block * gain).astype(bf16)
        if squared:
            square = jnp.broadcast_to(jnp.sum(block * block, axis=1, keepdims=True), (rows, HEAD_DIM))
            if place < half:
                keep[pl.ds(place, rows), pl.ds(0, HEAD_DIM)] = square
            else:
                upper = square.astype(bf16)
                send_ref[pl.ds(place - half, rows), pl.ds(0, HEAD_DIM)] = upper
                lower = (square - upper.astype(f32)).astype(bf16)
                send_ref[pl.ds(place - half, rows), pl.ds(HEAD_DIM, HEAD_DIM)] = lower
    stores = []
    for at, (copy, (begin, width)) in enumerate(zip(copies, tiles)):
        copy.wait()
        if at + IN_FLIGHT < len(copies):
            copies[at + IN_FLIGHT].start()
        total = jnp.dot(acts[...], w[:, pl.ds(begin, width)], preferred_element_type=f32)
        keep[:, pl.ds(offset + begin, width)] = total[:half]
        send_ref[:, pl.ds(2 * offset + begin, width)] = total[half:].astype(bf16)
        left = 0 if at == 0 else offset + begin
        columns = pl.ds(left, offset + begin + width - left)
        store = pltpu.make_async_copy(keep.at[:, columns], keep_hbm.at[:, columns], keep_sems.at[at])
        store.start()
        stores.append(store)
    for store in stores:
        store.wait()


def tiles_of(width):
    sizes = [256] if width % 256 == 0 else []
    while width > sum(sizes):
        sizes.append(min(512, width - sum(sizes)))
    return tuple((sum(sizes[:i]), size) for i, size in enumerate(sizes))


def project(z, a0, a1, gain, weight, rows, first, width, squared):
    depth = a0.shape[1]
    kept = a0.shape[0] // rows // 2
    half = kept * CORES * rows
    tiles = tiles_of(width)
    full = width + (HEAD_DIM if squared else 0)
    vmem = pl.BlockSpec(memory_space=pltpu.VMEM)
    hbm = pl.BlockSpec(memory_space=pltpu.HBM)
    return pl.pallas_call(
        functools.partial(project_kernel, rows, kept, first, tiles, squared),
        out_shape=(
            jax.ShapeDtypeStruct((half, full), f32),
            jax.ShapeDtypeStruct((half, 2 * full - width), bf16),
        ),
        in_specs=[pl.BlockSpec(memory_space=pltpu.SMEM), hbm, hbm, vmem, hbm],
        out_specs=(hbm, vmem),
        scratch_shapes=[
            pltpu.VMEM((2 * half, depth), bf16),
            pltpu.VMEM((2 * half, depth), bf16),
            pltpu.VMEM((depth, width), bf16),
            pltpu.VMEM((half, full), f32),
            pltpu.SemaphoreType.DMA((2 * kept * CORES,)),
            pltpu.SemaphoreType.DMA((len(tiles),)),
            pltpu.SemaphoreType.DMA((len(tiles),)),
        ],
        compiler_params=pltpu.CompilerParams(vmem_limit_bytes=32 * 2**20),
        name="project",
    )(z, a0, a1, gain, weight)


def attend_kernel(plan, rows, per_source, *refs):
    count = len(plan)
    places_ref, lengths_ref, cosine_ref, sine_ref = refs[:4]
    pieces = refs[4 : 4 + count]
    keys, values, _, attended_ref, cache_rows_ref = refs[4 + count : 9 + count]
    heads, scores_ref, weights_ref, mixed = refs[9 + count :]
    cosine = cosine_ref[...]
    sine = sine_ref[...]
    rotated = HEADS + KV_HEADS
    for (source, first, width, start), piece in zip(plan, pieces):
        for column in range(0, width, HEAD_DIM):
            local = (first + column) // HEAD_DIM
            h = places_ref[source] * per_source + local
            head = piece[pl.ds(start, rows), pl.ds(column, HEAD_DIM)].astype(f32)
            turned = head * cosine + pltpu.roll(head, HEAD_DIM // 2, 1) * sine
            if local + KV_HEADS >= per_source:
                turned = jnp.where(h < rotated, turned, head)
            heads[pl.ds(pl.multiple_of(h * rows, rows), rows), :] = turned.astype(bf16).astype(f32)
    for h in range(2 * KV_HEADS):
        cache_rows_ref[:, pl.ds(h * HEAD_DIM, HEAD_DIM)] = heads[pl.ds((HEADS + h) * rows, rows), :].astype(bf16)
    span = keys.shape[1]
    position = lax.broadcasted_iota(jnp.int32, (HEADS, span), 1)

    def score(r):
        query = heads[pl.ds(r, HEADS, stride=rows), :].astype(bf16)
        empty = jnp.zeros((GROUP, HEAD_DIM), bf16)
        for k in range(0, KV_HEADS, 2):
            front = jnp.concatenate([query[k * GROUP : (k + 1) * GROUP], empty], axis=1)
            second = jnp.concatenate([empty, query[(k + 1) * GROUP : (k + 2) * GROUP]], axis=1)
            scores_ref[r, pl.ds(k * GROUP, 2 * GROUP), :] = lax.dot_general(
                jnp.concatenate([front, second], axis=0),
                keys[r, :, pl.ds(k * HEAD_DIM, 2 * HEAD_DIM)],
                (((1,), (1,)), ((), ())),
                preferred_element_type=f32,
            )

    def soften(r):
        query = heads[pl.ds(r, HEADS, stride=rows), :]
        own_key = heads[pl.ds(HEADS * rows + r, KV_HEADS, stride=rows), :]
        own_value = heads[pl.ds((HEADS + KV_HEADS) * rows + r, KV_HEADS, stride=rows), :]
        spread = jnp.concatenate(
            [jnp.broadcast_to(own_key[k : k + 1], (GROUP, HEAD_DIM)) for k in range(KV_HEADS)], axis=0
        )
        own_score = jnp.sum(query * spread, axis=1, keepdims=True) * HEAD_DIM ** (-0.5)
        masked = jnp.where(position < lengths_ref[r], scores_ref[r] * HEAD_DIM ** (-0.5), -jnp.inf)
        top = jnp.maximum(jnp.max(masked, axis=1, keepdims=True), own_score)
        raised = jnp.exp(masked - top)
        raised_own = jnp.exp(own_score - top)
        inverse = 1.0 / (jnp.sum(raised, axis=1, keepdims=True) + raised_own)
        weights_ref[r] = (raised * inverse).astype(bf16)
        own_weight = (raised_own * inverse).astype(bf16).astype(f32)
        spread = jnp.concatenate(
            [jnp.broadcast_to(own_value[k : k + 1], (GROUP, HEAD_DIM)) for k in range(KV_HEADS)], axis=0
        )
        scores_ref[r] = own_weight * spread

    def mix(r):
        for k in range(0, KV_HEADS, 2):
            both = jnp.dot(
                weights_ref[r, pl.ds(k * GROUP, 2 * GROUP), :],
                values[r, :, pl.ds(k * HEAD_DIM, 2 * HEAD_DIM)],
                preferred_element_type=f32,
            )
            for i in range(2):
                mixed[pl.ds((k + i) * GROUP * rows + r, GROUP, stride=rows), :] = (
                    both[i * GROUP : (i + 1) * GROUP, i * HEAD_DIM : (i + 1) * HEAD_DIM]
                    + scores_ref[r, pl.ds((k + i) * GROUP, GROUP), :]
                )

    for r in range(rows):
        score(r)
    for r in range(rows):
        soften(r)
    for r in range(rows):
        mix(r)
    for h in range(HEADS):
        attended_ref[:, pl.ds(h * HEAD_DIM, HEAD_DIM)] = mixed[pl.ds(h * rows, rows), :].astype(bf16)


def attend(plan, pieces, places, lengths, cosine, sine, key_cache, value_cache, fetched, width):
    rows, span, kv_width = key_cache.shape
    smem = pl.BlockSpec(memory_space=pltpu.SMEM)
    vmem = pl.BlockSpec(memory_space=pltpu.VMEM)
    return pl.pallas_call(
        functools.partial(attend_kernel, plan, rows, width // HEAD_DIM),
        out_shape=(
            jax.ShapeDtypeStruct((rows, HEADS * HEAD_DIM), bf16),
            jax.ShapeDtypeStruct((rows, 2 * KV_HEADS * HEAD_DIM), bf16),
        ),
        in_specs=[smem, smem] + [vmem] * (len(pieces) + 5),
        out_specs=(vmem, vmem),
        scratch_shapes=[
            pltpu.VMEM(((HEADS + 2 * KV_HEADS) * rows, HEAD_DIM), f32),
            pltpu.VMEM((rows, HEADS, span), f32),
            pltpu.VMEM((rows, HEADS, span), bf16),
            pltpu.VMEM((HEADS * rows, HEAD_DIM), f32),
        ],
        compiler_params=pltpu.CompilerParams(vmem_limit_bytes=12 * 2**20),
        name="attend",
    )(places, lengths, cosine, sine, *pieces, key_cache, value_cache, fetched)


def fetch_kernel(keys_hbm, values_hbm, keys, values, fetched, sems):
    loads = [
        pltpu.make_async_copy(keys_hbm, keys, sems.at[0]),
        pltpu.make_async_copy(values_hbm, values, sems.at[1]),
    ]
    for load in loads:
        load.start()
    for load in loads:
        load.wait()
    fetched[...] = jnp.zeros_like(fetched)


def fetch(key_cache, value_cache):
    vmem = pl.BlockSpec(memory_space=pltpu.VMEM)
    hbm = pl.BlockSpec(memory_space=pltpu.HBM)
    shape = jax.ShapeDtypeStruct(key_cache.shape, bf16)
    return pl.pallas_call(
        fetch_kernel,
        out_shape=(shape, shape, jax.ShapeDtypeStruct((8, 128), f32)),
        in_specs=[hbm, hbm],
        out_specs=(vmem, vmem, vmem),
        scratch_shapes=[pltpu.SemaphoreType.DMA((2,))],
        compiler_params=pltpu.CompilerParams(vmem_limit_bytes=16 * 2**20),
        name="fetch",
    )(key_cache, value_cache)


def rotation(lengths):
    half = HEAD_DIM // 2
    steps = jnp.arange(half, dtype=f32)
    inverse = jnp.exp(steps * (-2.0 * math.log(rope_base) / HEAD_DIM))
    angles = lengths.astype(f32)[:, None] * inverse[None, :]
    cosine = jnp.cos(angles)
    sine = jnp.sin(angles)
    return jnp.concatenate([cosine, cosine], axis=1), jnp.concatenate([-sine, sine], axis=1)


def body(hidden_states, norm_gain, projection_weight, key_cache, value_cache, lengths):
    along_x = lax.axis_size("gx")
    along_z = lax.axis_size("gy")
    chips = along_x // CORES
    rows = key_cache.shape[0]
    width = projection_weight.shape[1]
    z = lax.axis_index("gy").reshape(1).astype(jnp.int32)
    gx = lax.axis_index("gx")
    kept = along_z // 2
    first_rows = CORES * rows

    def on_gx(array, shift, flip):
        pairs = [
            ((x + shift) % chips * CORES + (c ^ flip), x * CORES + c)
            for x in range(chips)
            for c in range(CORES)
        ]
        return lax.ppermute(array, "gx", pairs)

    def on_z(array, flip):
        return lax.ppermute(array, "gy", [(s, s ^ flip) for s in range(along_z)])

    def in_hbm(array):
        return pltpu.with_memory_space_constraint(array, pltpu.HBM)

    gain = norm_gain.reshape(1, -1)
    weight = in_hbm(projection_weight)
    there = [on_gx(hidden_states, k, 0) for k in range(1, chips)]
    here = [(in_hbm(hidden_states), on_gx(hidden_states, 0, 1))]
    cosine, sine = rotation(lengths)

    unit = HEAD_DIM * 2
    if width % unit == 0 and width >= 4 * unit:
        own_cut, other_cut = split_at(width, unit, OWN_SHARE), split_at(width, unit, OTHER_SHARE)
    else:
        own_cut = other_cut = (width,)
    units = [(0, 0, own_cut[0], True)]
    for k in range(1, chips):
        units.append((k, 0, other_cut[0], True))
        units += [(k, other_cut[0], rest, False) for rest in other_cut[1:]]
    units += [(0, own_cut[0], rest, False) for rest in own_cut[1:]]

    def tie(*arrays):
        return lax.optimization_barrier(arrays)

    count = len(units)
    keeps, receiveds, owns, aways, arrived = [], [], [], [], []

    def add_pair(keep, received, squared):
        results = []
        for rest in (False, True):
            span = slice(first_rows, None) if rest else slice(0, first_rows)
            skip = HEAD_DIM if squared else 0
            parts = []
            if squared:
                square = (
                    keep[span, :HEAD_DIM]
                    + received[span, :HEAD_DIM].astype(f32)
                    + received[span, HEAD_DIM : 2 * HEAD_DIM].astype(f32)
                )
                upper = lax.reduce_precision(square, 8, 7)
                parts = [upper.astype(bf16), (square - upper).astype(bf16)] if rest else [square]
            total = keep[span, skip:] + received[span, 2 * skip :].astype(f32)
            results.append(parts + [total.astype(bf16) if rest else total])
        return results

    def step_one(u):
        own, away = add_pair(keeps[u], receiveds[u], units[u][3])
        owns.append(own)
        aways.append(jnp.concatenate(away, axis=1) if len(away) > 1 else away[0])

    def step_two(u):
        away = aways[u]
        arrived.append([on_z(away[(i - 1) * first_rows : i * first_rows], 2 * i) for i in range(1, kept)])

    sides = {0: here[0]}
    for u, (k, first, chunk, squared) in enumerate(units):
        if u > 1:
            receiveds[u - 2], keeps[u - 1] = tie(receiveds[u - 2], keeps[u - 1])
        if k not in sides:
            array, keeps[u - 1] = tie(there[k - 1], keeps[u - 1])
            sides[k] = (array, on_gx(array, 0, 1))
        a0, a1 = sides[k]
        if u:
            a0, keeps[u - 1] = tie(a0, keeps[u - 1])
        if u > 1:
            step_one(u - 2)
            a0, aways[u - 2] = tie(a0, aways[u - 2])
            step_two(u - 2)
        if u > 2:
            a0, arrived[u - 3] = tie(a0, arrived[u - 3])
        sides[k] = (a0, a1)
        keep, send = project(z, a0, a1, gain, weight, rows, first, chunk, squared)
        keeps.append(keep)
        receiveds.append(on_z(send, 1))
    plan, pieces, scales, projecteds = [], [], {}, []

    def finish(u):
        k, first, chunk, squared = units[u]
        own, others = owns[u], arrived[u]
        skip = 2 * HEAD_DIM if squared else 0
        if squared:
            square = own[0]
            for other in others:
                square = square + other[:, :HEAD_DIM].astype(f32) + other[:, HEAD_DIM:skip].astype(f32)
            scales[k] = lax.rsqrt(square[:, :1] * (1.0 / D) + norm_eps)
        total = own[-1]
        for other in others:
            total = total + other[:, skip:].astype(f32)
        projecteds.append((total * scales[k]).astype(bf16))

    def hand_out(u):
        k, first, chunk, _ = units[u]
        plan.append((k * CORES, first, chunk, 0))
        plan.append((k * CORES + 1, first, chunk, rows))
        held.append(on_gx(projecteds[u], chips - k, 0) if k else projecteds[u])

    held = []
    last = count - 1
    if count > 1:
        u = last - 1
        if u:
            receiveds[u], keeps[last], arrived[u - 1] = tie(receiveds[u], keeps[last], arrived[u - 1])
        step_one(u)
        *arrived[:], aways[u] = tie(*arrived, aways[u])
        step_two(u)
        for before in range(u):
            finish(before)
            hand_out(before)
        if u:
            receiveds[last], projecteds[-1], aways[u] = tie(receiveds[last], projecteds[-1], aways[u])
    step_one(last)
    if count > 1:
        arrived[last - 1], aways[last] = tie(arrived[last - 1], aways[last])
    step_two(last)
    if count > 1:
        finish(last - 1)
        hand_out(last - 1)
        projecteds[-1], key_cache = tie(projecteds[-1], key_cache)
    keys, values, fetched = fetch(in_hbm(key_cache), in_hbm(value_cache))
    *held[: last - 1], arrived[last], fetched = tie(*held[: last - 1], arrived[last], fetched)
    finish(last)
    hand_out(last)
    for projected in held:
        pieces.append(projected)
        pieces.append(on_gx(projected, 0, 1))
    x, core = gx // CORES, gx % CORES
    places = jnp.stack(
        [
            (x + chips - k) % chips * CORES + jnp.bitwise_xor(core, j)
            for k in range(chips)
            for j in range(CORES)
        ]
    ).astype(jnp.int32)
    return attend(
        plan, pieces, places, lengths, cosine, sine, keys, values, fetched, width
    )


def split_at(width, unit, share):
    first = round(width * share / unit) * unit
    return (first, width - first)


def solution(mesh):
    in_specs = (
        P(("groups", "gx"), "gy"),
        P("gy"),
        P("gy", "gx"),
        P(("groups", "gx", "gy"), None, None),
        P(("groups", "gx", "gy"), None, None),
        P(("groups", "gx", "gy")),
    )
    out_specs = (P(("groups", "gx", "gy"), None), P(("groups", "gx", "gy"), None))
    return jax.shard_map(body, mesh=mesh, in_specs=in_specs, out_specs=out_specs, check_vma=False)
```
